32 devices in a mesh: seq: 8 (over y, x, core), sub: 4 (over z).
Axes of the slice: x: 2, y: 2, z: 4, core: 2. Of those that a mesh axis runs over, the one named last changes fastest.
Arguments:
- video: bfloat16 [4096, 1536], P(('seq', 'sub')), may hold values from -6 to 6
- conditioning: bfloat16 [5, 1024], replicated, may hold values from -6 to 6
- captions: bfloat16 [1280, 4096], P('sub'), may hold values from -6 to 6
- clip_lengths: int32 [5], replicated, may hold values from 1 to 2048, 4096 in all
- cap_lengths: int32 [5], replicated, may hold values from 64 to 256, as said below
- positions: int32 [4096, 3], P(('seq', 'sub')), may hold values from 0 to 63
- ada_weight: bfloat16 [1024, 6144], P(('seq', 'sub')), may hold values from -0.1875 to 0.1875
- ada_bias: bfloat16 [6144], P(('seq', 'sub')), may hold values from -3 to 3
- query_weight: bfloat16 [1536, 1536], P(('seq', 'sub')), may hold values from -0.15625 to 0.15625
- key_weight: bfloat16 [1536, 1536], P(('seq', 'sub')), may hold values from -0.15625 to 0.15625
- value_weight: bfloat16 [1536, 1536], P(('seq', 'sub')), may hold values from -0.15625 to 0.15625
- out_weight: bfloat16 [1536, 1536], P(('seq', 'sub')), may hold values from -0.15625 to 0.15625
- text_key_weight: bfloat16 [4096, 1536], P(('seq', 'sub')), may hold values from -0.09375 to 0.09375
- text_value_weight: bfloat16 [4096, 1536], P(('seq', 'sub')), may hold values from -0.09375 to 0.09375
- gate_weight: bfloat16 [1536, 4096], P(('seq', 'sub')), may hold values from -0.15625 to 0.15625
- up_weight: bfloat16 [1536, 4096], P(('seq', 'sub')), may hold values from -0.15625 to 0.15625
- down_weight: bfloat16 [4096, 1536], P(('seq', 'sub')), may hold values from -0.09375 to 0.09375
- attn_gain: bfloat16 [1536], P(('seq', 'sub')), may hold values from 0.5 to 1.5
- query_gain: bfloat16 [1536], P(('seq', 'sub')), may hold values from 0.5 to 1.5
- key_gain: bfloat16 [1536], P(('seq', 'sub')), may hold values from 0.5 to 1.5
- text_key_gain: bfloat16 [1536], P(('seq', 'sub')), may hold values from 0.5 to 1.5
- attn_out_gain: bfloat16 [1536], P(('seq', 'sub')), may hold values from 0.5 to 1.5
- ffn_gain: bfloat16 [1536], P(('seq', 'sub')), may hold values from 0.5 to 1.5
- ffn_out_gain: bfloat16 [1536], P(('seq', 'sub')), may hold values from 0.5 to 1.5
- cross_gate: bfloat16 [24], replicated, may hold values from -1.5 to 1.5
- cotangent: bfloat16 [4096, 1536], P(('seq', 'sub')), may hold values from -6 to 6
Outputs:
- block_out: bfloat16 [4096, 1536], P(('seq', 'sub'))
- video_grad: float32 [4096, 1536], P(('seq', 'sub'))
- caption_grad: float32 [1280, 4096], P('sub')
- cond_grad: float32 [5, 1024], replicated
- ada_weight_grad: float32 [1024, 6144], P(('seq', 'sub'))
- ada_bias_grad: float32 [6144], P(('seq', 'sub'))
- query_weight_grad: float32 [1536, 1536], P(('seq', 'sub'))
- key_weight_grad: float32 [1536, 1536], P(('seq', 'sub'))
- value_weight_grad: float32 [1536, 1536], P(('seq', 'sub'))
- out_weight_grad: float32 [1536, 1536], P(('seq', 'sub'))
- text_key_weight_grad: float32 [4096, 1536], P(('seq', 'sub'))
- text_value_weight_grad: float32 [4096, 1536], P(('seq', 'sub'))
- gate_weight_grad: float32 [1536, 4096], P(('seq', 'sub'))
- up_weight_grad: float32 [1536, 4096], P(('seq', 'sub'))
- down_weight_grad: float32 [4096, 1536], P(('seq', 'sub'))
- attn_gain_grad: float32 [1536], P(('seq', 'sub'))
- query_gain_grad: float32 [1536], P(('seq', 'sub'))
- key_gain_grad: float32 [1536], P(('seq', 'sub'))
- text_key_gain_grad: float32 [1536], P(('seq', 'sub'))
- attn_out_gain_grad: float32 [1536], P(('seq', 'sub'))
- ffn_gain_grad: float32 [1536], P(('seq', 'sub'))
- ffn_out_gain_grad: float32 [1536], P(('seq', 'sub'))
- cross_gate_grad: float32 [24], replicated
The draws below stay inside these ranges and needn't reach their ends.
Inputs may be any that keep to these rules, and one draw needn't show every extreme that they name: `clip_lengths`: clip lengths sum to 4096; the longest clip has exactly 2048 tokens. `cap_lengths`: one clip's caption fills all 256 slots.
All inputs are finite; a program needn't handle non-finite values.
Results may differ from the reference program's by a relative error of at most 0.04.
Values may be sent and summed in bfloat16 or wider, within the bound.
No kernel may reach another device: no remote copies, remote signals or barrier semaphores. Data moves between devices by JAX's collectives and lax.ppermute only.
A program may use at most 384 MiB of HBM per device.

```python
import math
import jax
import jax.numpy as jnp
import numpy as np
from jax import lax

D = 1536
H = 24
HD = 64
FF = 4096
TD = 4096
COND = 1024
CLIPS = 5
CAP = 256
TOKENS = 4096
CAPTOK = 1280


def draw_cap_lengths(key, part):
    key_draw, key_pick = jax.random.split(jax.random.fold_in(key, 17))
    lengths_drawn = jax.random.randint(key_draw, (CLIPS,), CAP // 4, CAP + 1)
    chosen = jax.random.randint(key_pick, (), 0, CLIPS)
    return jnp.where(jnp.arange(CLIPS) == chosen, CAP, lengths_drawn).astype(jnp.int32)


def place_ends(entries, rng, least, largest):
    longest = entries.shape.index(max(entries.shape))
    spots = []
    for shift in (0, 1):
        where = [jax.random.randint(jax.random.fold_in(rng, axis), (), 0, length) for axis, length in enumerate(entries.shape)]
        where[longest] = (where[longest] + shift) % entries.shape[longest]
        spots.append(tuple(where))
    return entries.at[spots[0]].set(least).at[spots[1]].set(largest)


def levels(own_key, extent, cuts, smallest, high):
    loudness, own = 1.0, jax.random.fold_in(own_key, 6)
    for position, blocks in cuts:
        steps = jnp.exp(jax.random.uniform(jax.random.fold_in(own, position), (blocks,), jnp.float32, smallest / len(cuts), high / len(cuts)))
        loudness = loudness * jnp.repeat(steps, extent[position] // blocks).reshape([-1 if axis == position else 1 for axis in range(len(extent))])
    return loudness


def profile(number_of, total, reach, skew):
    weights = [(1 << 20) // math.isqrt(grade ** skew) + 1 for grade in range(2, number_of + 1)]
    surplus, counts = total - reach - (number_of - 1), [1] * (number_of - 1)
    while surplus > 0:
        movable = [i for i in range(number_of - 1) if counts[i] < reach]
        mass, remaining = sum([weights[i] for i in movable]), surplus
        for i in movable:
            more = min(reach - counts[i], max(1, remaining * weights[i] // mass), surplus)
            counts[i] = counts[i] + more
            surplus = surplus - more
    return np.array([reach] + counts)


def ragged(key, number_of, total, bound, lean):
    if number_of == 2:
        one = jax.random.randint(key, (), max(1, total - bound), min(bound, total - 1) + 1)
        return jnp.stack([one, total - one])
    sizes = jnp.asarray(profile(number_of, total, bound, lean), jnp.int32)
    twos = (number_of - 1) // 2
    source_of, taker = sizes[1:1 + 2 * twos:2], sizes[2:2 + 2 * twos:2]
    margin = jnp.minimum(source_of - 1, bound - taker)
    moved = jax.random.randint(jax.random.fold_in(key, 1), (twos,), 0, 1 << 20) % (margin + 1)
    sizes = sizes.at[1:1 + 2 * twos:2].set(source_of - moved).at[2:2 + 2 * twos:2].set(taker + moved)
    return sizes[jax.random.permutation(jax.random.fold_in(key, 2), number_of)]


def scatter_about(own_key, shape, scale, reach, cuts=(), kind=jnp.bfloat16):
    values = jax.random.normal(own_key, shape, jnp.float32) * scale
    if len(cuts) > 0:
        values = levels(own_key, shape, cuts, -0.22, 0.18) * values
    return jnp.clip(values, min=-reach, max=reach).astype(kind)


def setup_inputs(seed: int = 0) -> dict:
    keys = jax.random.split(jax.random.key(seed), 27)
    video = scatter_about(keys[0], (TOKENS, D), 1.0, 6.0, ((0, 32),))
    conditioning = scatter_about(keys[1], (CLIPS, COND), 1.0, 6.0)
    captions = scatter_about(keys[2], (CAPTOK, TD), 1.0, 6.0, ((0, 4),))
    clip_lengths = ragged(keys[3], CLIPS, TOKENS, TOKENS // 2, 2).astype(jnp.int32)
    cap_lengths = draw_cap_lengths(jax.random.fold_in(keys[26], 71), 0)
    positions = place_ends(jax.random.randint(keys[5], (TOKENS, 3), 0, 64), jax.random.fold_in(keys[5], 1), 0, 63).astype(jnp.int32)
    ada_weight = scatter_about(keys[6], (COND, 4 * D), COND ** -0.5, 0.1875, ((0, 32),))
    ada_bias = scatter_about(keys[7], (4 * D,), 0.5, 3.0, ((0, 32),))
    query_weight = scatter_about(keys[8], (D, D), D ** -0.5, 0.15625, ((0, 32),))
    key_weight = scatter_about(keys[9], (D, D), D ** -0.5, 0.15625, ((0, 32),))
    value_weight = scatter_about(keys[10], (D, D), D ** -0.5, 0.15625, ((0, 32),))
    out_weight = scatter_about(keys[11], (D, D), D ** -0.5, 0.15625, ((0, 32),))
    text_key_weight = scatter_about(keys[12], (TD, D), TD ** -0.5, 0.09375, ((0, 32),))
    text_value_weight = scatter_about(keys[13], (TD, D), TD ** -0.5, 0.09375, ((0, 32),))
    gate_weight = scatter_about(keys[14], (D, FF), D ** -0.5, 0.15625, ((0, 32),))
    up_weight = scatter_about(keys[15], (D, FF), D ** -0.5, 0.15625, ((0, 32),))
    down_weight = scatter_about(keys[16], (FF, D), FF ** -0.5, 0.09375, ((0, 32),))
    attn_gain = jnp.clip(1.0 + 0.1 * jax.random.normal(keys[17], (D,), jnp.float32), 0.5, 1.5).astype(jnp.bfloat16)
    query_gain = jnp.clip(1.0 + 0.1 * jax.random.normal(keys[18], (D,), jnp.float32), 0.5, 1.5).astype(jnp.bfloat16)
    key_gain = jnp.clip(1.0 + 0.1 * jax.random.normal(keys[19], (D,), jnp.float32), 0.5, 1.5).astype(jnp.bfloat16)
    text_key_gain = jnp.clip(1.0 + 0.1 * jax.random.normal(keys[20], (D,), jnp.float32), 0.5, 1.5).astype(jnp.bfloat16)
    attn_out_gain = jnp.clip(1.0 + 0.1 * jax.random.normal(keys[21], (D,), jnp.float32), 0.5, 1.5).astype(jnp.bfloat16)
    ffn_gain = jnp.clip(1.0 + 0.1 * jax.random.normal(keys[22], (D,), jnp.float32), 0.5, 1.5).astype(jnp.bfloat16)
    ffn_out_gain = jnp.clip(1.0 + 0.1 * jax.random.normal(keys[23], (D,), jnp.float32), 0.5, 1.5).astype(jnp.bfloat16)
    cross_gate = jnp.clip(jax.random.uniform(keys[24], (H,), jnp.float32, -1.5, 1.5), -1.5, 1.5).astype(jnp.bfloat16)
    cotangent = scatter_about(keys[25], (TOKENS, D), 1.0, 6.0, ((0, 32),))
    return {"video": video, "conditioning": conditioning, "captions": captions, "clip_lengths": clip_lengths, "cap_lengths": cap_lengths, "positions": positions, "ada_weight": ada_weight, "ada_bias": ada_bias, "query_weight": query_weight, "key_weight": key_weight, "value_weight": value_weight, "out_weight": out_weight, "text_key_weight": text_key_weight, "text_value_weight": text_value_weight, "gate_weight": gate_weight, "up_weight": up_weight, "down_weight": down_weight, "attn_gain": attn_gain, "query_gain": query_gain, "key_gain": key_gain, "text_key_gain": text_key_gain, "attn_out_gain": attn_out_gain, "ffn_gain": ffn_gain, "ffn_out_gain": ffn_out_gain, "cross_gate": cross_gate, "cotangent": cotangent}


epsilon = 1e-06
rope_base = 10000.0
masked_score = -1e+30
highest = lax.Precision.HIGHEST

@jax.custom_vjp
def low(v):
    return lax.optimization_barrier(v.astype(jnp.bfloat16)).astype(jnp.float32)

@jax.custom_vjp
def low_back(v):
    return v

def low_keep(v):
    return (low(v), None)

def low_pass(kept, grad):
    return (grad,)

def back_keep(v):
    return (v, None)

def back_low(kept, grad):
    return (low(grad),)
low.defvjp(low_keep, low_pass)
low_back.defvjp(back_keep, back_low)

def rms_norm(values):
    return values * lax.rsqrt(lax.optimization_barrier(jnp.mean(values * values, -1, keepdims=True)) + epsilon)

def rope_tables(positions, head_dim):
    pair_total = head_dim // 2
    frame_pairs = pair_total // 4
    height_pairs = (pair_total - frame_pairs) // 2
    width_pairs = pair_total - frame_pairs - height_pairs
    pieces = []
    for axis_id, pair_count in enumerate((frame_pairs, height_pairs, width_pairs)):
        frequency = rope_base ** (-jnp.arange(pair_count, dtype=jnp.float32) / pair_count)
        pieces.append(positions[:, axis_id].astype(jnp.float32)[:, None] * frequency[None, :])
    angles = jnp.concatenate(pieces, 1)
    return (jnp.cos(angles), jnp.sin(angles))

def rotate(values, cosine, sine):
    shaped = values.reshape(values.shape[0], values.shape[1], -1, 2)
    even_part = shaped[..., 0]
    odd_part = shaped[..., 1]
    cos_part = cosine[:, None, :]
    sin_part = sine[:, None, :]
    turned = jnp.stack([even_part * cos_part - odd_part * sin_part, even_part * sin_part + odd_part * cos_part], -1)
    return turned.reshape(values.shape)

def clip_index(token_index, clip_lengths):
    bounds = jnp.cumsum(clip_lengths)
    return lax.optimization_barrier(jnp.sum((token_index[:, None] >= bounds[None, :]).astype(jnp.int32), 1))

def attend(queries, key_rows, values, query_clip, key_clip, key_valid):
    rows_total = queries.shape[0]
    block_rows = min(256, rows_total)
    query_blocks = queries.reshape(rows_total // block_rows, block_rows, queries.shape[1], queries.shape[2])
    clip_blocks = query_clip.reshape(rows_total // block_rows, block_rows)

    def one_block(inputs):
        query_blk, clip_blk = inputs
        scores = low_back(jnp.einsum('qhd,khd->qhk', query_blk, key_rows, precision=highest) / math.sqrt(queries.shape[2]))
        allowed = ((clip_blk[:, None] == key_clip[None, :]) & key_valid[None, :])[:, None, :]
        weights = low(jax.nn.softmax(jnp.where(allowed, scores, masked_score), -1))
        return jnp.einsum('qhk,khd->qhd', weights, values, precision=highest)
    result = lax.map(jax.checkpoint(one_block), (query_blocks, clip_blocks))
    return result.reshape(queries.shape)

def reference(video, conditioning, captions, clip_lengths, cap_lengths, positions, ada_weight, ada_bias, query_weight, key_weight, value_weight, out_weight, text_key_weight, text_value_weight, gate_weight, up_weight, down_weight, attn_gain, query_gain, key_gain, text_key_gain, attn_out_gain, ffn_gain, ffn_out_gain, cross_gate, cotangent):
    token_clip = clip_index(jnp.arange(TOKENS, dtype=jnp.int32), clip_lengths)
    cap_row = jnp.arange(CAPTOK, dtype=jnp.int32)
    caption_clip = cap_row // CAP
    caption_valid = cap_row % CAP < cap_lengths[caption_clip]
    all_valid = jnp.ones((TOKENS,), jnp.bool_)
    cosine, sine = rope_tables(positions, HD)

    def forward(video_in, cond_in, caption_in, ada_w, ada_b, query_w, key_w, value_w, out_w, text_key_w, text_value_w, gate_w, up_w, down_w, attn_g, query_g, key_g, text_key_g, attn_out_g, ffn_g, ffn_out_g, gate_h):
        modulation = low_back(jnp.dot(low(jax.nn.silu(cond_in)), ada_w, precision=highest) + ada_b)
        per_token = modulation[token_clip]
        attn_scale = per_token[:, :D]
        attn_gate = per_token[:, D:2 * D]
        ffn_scale = per_token[:, 2 * D:3 * D]
        ffn_gate = per_token[:, 3 * D:]
        normed = low(rms_norm(video_in) * attn_g * (1.0 + attn_scale))
        query_pre = low_back(jnp.dot(normed, query_w, precision=highest))
        key_pre = low_back(jnp.dot(normed, key_w, precision=highest))
        values = low_back(low(jnp.dot(normed, value_w, precision=highest))).reshape(TOKENS, H, HD)
        queries = low_back(low(rotate((rms_norm(query_pre) * query_g).reshape(TOKENS, H, HD), cosine, sine)))
        key_rows = low_back(low(rotate((rms_norm(key_pre) * key_g).reshape(TOKENS, H, HD), cosine, sine)))
        text_key_pre = low_back(jnp.dot(caption_in, text_key_w, precision=highest))
        text_keys = low_back(low(rms_norm(text_key_pre) * text_key_g)).reshape(CAPTOK, H, HD)
        text_values = low_back(low(jnp.dot(caption_in, text_value_w, precision=highest))).reshape(CAPTOK, H, HD)
        self_out = low(attend(queries, key_rows, values, token_clip, token_clip, all_valid))
        cross_out = low_back(attend(queries, text_keys, text_values, token_clip, caption_clip, caption_valid))
        mixed = low_back(low((self_out + jnp.tanh(gate_h)[None, :, None] * cross_out).reshape(TOKENS, D)))
        projected = low_back(jnp.dot(mixed, out_w, precision=highest))
        hidden_state = video_in + jnp.tanh(attn_gate) * rms_norm(projected) * attn_out_g
        ffn_in = low(rms_norm(hidden_state) * ffn_g * (1.0 + ffn_scale))
        gate_pre = low_back(jnp.dot(ffn_in, gate_w, precision=highest))
        up_pre = low_back(jnp.dot(ffn_in, up_w, precision=highest))
        activated = low(jax.nn.silu(gate_pre) * up_pre)
        down_out = low_back(jnp.dot(activated, down_w, precision=highest))
        return hidden_state + jnp.tanh(ffn_gate) * rms_norm(down_out) * ffn_out_g
    params = tuple((array_in.astype(jnp.float32) for array_in in (video, conditioning, captions, ada_weight, ada_bias, query_weight, key_weight, value_weight, out_weight, text_key_weight, text_value_weight, gate_weight, up_weight, down_weight, attn_gain, query_gain, key_gain, text_key_gain, attn_out_gain, ffn_gain, ffn_out_gain, cross_gate)))
    result, pullback = jax.vjp(forward, *params)
    gradients = pullback(cotangent.astype(jnp.float32))
    return (result.astype(jnp.bfloat16), gradients[0], gradients[2], gradients[1], gradients[3], gradients[4], gradients[5], gradients[6], gradients[7], gradients[8], gradients[9], gradients[10], gradients[11], gradients[12], gradients[13], gradients[14], gradients[15], gradients[16], gradients[17], gradients[18], gradients[19], gradients[20], gradients[21])
```

```python
import functools
import math

import jax
import jax.numpy as jnp
import numpy as np
from jax import lax
from jax.experimental import pallas as pl
from jax.experimental.pallas import tpu as pltpu
from jax.sharding import PartitionSpec as P

CAP = 256
KEY_BLOCK = 256
epsilon = 1e-06
rope_base = 10000.0
masked_score = -1e30
BF = jnp.bfloat16
F32 = jnp.float32
BOTH = ("seq", "sub")
VMEM_BYTES = 56 * 1024 * 1024


def xor_permute(values, axis, mask):
    count = lax.axis_size(axis)
    return lax.ppermute(values, axis, [(i, i ^ mask) for i in range(count)])


def axis_bits(axis):
    masks, mask = [], 1
    while mask < lax.axis_size(axis):
        masks.append(mask)
        mask *= 2
    return masks


def gather_cube(values, axis, order):
    index = lax.axis_index(axis)
    buffer = values[None]
    for mask in order:
        other = xor_permute(buffer, axis, mask)
        high = (index // mask) % 2 == 1
        buffer = jnp.stack([jnp.where(high, other, buffer), jnp.where(high, buffer, other)], 0)
    now = list(reversed(order))
    wanted = sorted(order, reverse=True)
    buffer = buffer.reshape((2,) * len(order) + values.shape)
    buffer = buffer.transpose(
        [now.index(mask) for mask in wanted] + list(range(len(order), buffer.ndim))
    )
    return buffer.reshape((-1,) + values.shape[1:])


def gather_seq(values):
    masks = axis_bits("seq")
    half = values.shape[-1] // 2
    first = masks[1:] + masks[:1]
    second = masks[1:][::-1] + masks[:1]
    return jnp.concatenate(
        [
            gather_cube(values[..., :half], "seq", first),
            gather_cube(values[..., half:], "seq", second),
        ],
        -1,
    )


def scatter_cube(values, axis, order):
    index = lax.axis_index(axis)
    count = lax.axis_size(axis)
    buffer = values.reshape((2,) * len(order) + (values.shape[0] // count,) + values.shape[1:])
    axes = sorted(order, reverse=True)
    for mask in order:
        place = axes.index(mask)
        bit = (index // mask) % 2
        mine = lax.dynamic_index_in_dim(buffer, bit, place, keepdims=False)
        send = lax.dynamic_index_in_dim(buffer, 1 - bit, place, keepdims=False)
        other = xor_permute(send, axis, mask)
        buffer = (mine.astype(F32) + other.astype(F32)).astype(values.dtype)
        axes.pop(place)
    return buffer


def scatter_seq(values):
    masks = axis_bits("seq")
    half = values.shape[-1] // 2
    first = masks[:1] + masks[1:]
    second = masks[:1] + masks[1:][::-1]
    return jnp.concatenate(
        [
            scatter_cube(values[..., :half], "seq", first),
            scatter_cube(values[..., half:], "seq", second),
        ],
        -1,
    )


def gather_line(values, axis):
    count = lax.axis_size(axis)
    index = lax.axis_index(axis)
    up = [(i, i + 1) for i in range(count - 1)]
    down = [(i + 1, i) for i in range(count - 1)]
    below, above = [], []
    from_below = from_above = values
    for _ in range(count - 1):
        from_below = lax.ppermute(from_below, axis, up)
        from_above = lax.ppermute(from_above, axis, down)
        below.append(from_below)
        above.append(from_above)
    line = jnp.concatenate(below[::-1] + [values] + above, 0)
    rows = values.shape[0]
    return lax.dynamic_slice_in_dim(line, (count - 1 - index) * rows, count * rows, 0)


def total(values, axes):
    for axis in axes:
        for mask in axis_bits(axis):
            values = values + xor_permute(values, axis, mask)
    return values


def swap_blocks(values, axis):
    return lax.all_to_all(values, axis, split_axis=0, concat_axis=0, tiled=True)


def gather_rows(values, axis):
    return lax.all_gather(values, axis, axis=0, tiled=True)


def scatter_rows(values, axis):
    return lax.psum_scatter(values, axis, scatter_dimension=0, tiled=True)


def inv_rms(values):
    return lax.rsqrt(jnp.mean(values * values, -1, keepdims=True) + epsilon)


def norm_back(normed_hat, inverse, grad_hat):
    return inverse * (grad_hat - normed_hat * jnp.mean(normed_hat * grad_hat, -1, keepdims=True))


def dot(left, right):
    return jnp.dot(left, right, preferred_element_type=F32)


def dot_nt(left, right):
    return lax.dot_general(left, right, (((1,), (1,)), ((), ())), preferred_element_type=F32)


def dot_tn(left, right):
    return lax.dot_general(left, right, (((0,), (0,)), ((), ())), preferred_element_type=F32)


def rope_tables(positions, head_dim, heads):
    pair_total = head_dim // 2
    frame_pairs = pair_total // 4
    height_pairs = (pair_total - frame_pairs) // 2
    width_pairs = pair_total - frame_pairs - height_pairs
    frequency = np.zeros((3, pair_total), np.float32)
    start = 0
    for axis_id, pair_count in enumerate((frame_pairs, height_pairs, width_pairs)):
        exponent = -np.arange(pair_count, dtype=np.float32) / np.float32(pair_count)
        frequency[axis_id, start : start + pair_count] = np.float32(rope_base) ** exponent
        start += pair_count
    frequency = jnp.asarray(np.repeat(frequency, 2, axis=1))
    angles = (
        positions[:, 0:1] * frequency[0:1]
        + positions[:, 1:2] * frequency[1:2]
        + positions[:, 2:3] * frequency[2:3]
    )
    sign = jnp.asarray(np.where(np.arange(head_dim) % 2 == 0, -1.0, 1.0).astype(np.float32))
    cosine = jnp.cos(angles)
    sine = jnp.sin(angles) * sign[None, :]
    return (jnp.tile(cosine, (1, heads)), jnp.tile(sine, (1, heads)))


def rotate(values, cosine, sine):
    even = lax.broadcasted_iota(jnp.int32, values.shape, 1) % 2 == 0
    swapped = jnp.where(even, jnp.roll(values, -1, 1), jnp.roll(values, 1, 1))
    return values * cosine + swapped * sine


def clip_index(token_index, clip_lengths):
    bounds = jnp.cumsum(clip_lengths)
    return jnp.sum((token_index[:, None] >= bounds[None, :]).astype(jnp.int32), 1)


def pick_rows(onehot, rows):
    picked = onehot[:, 0:1] * rows[0:1]
    for clip in range(1, rows.shape[0]):
        picked = picked + onehot[:, clip : clip + 1] * rows[clip : clip + 1]
    return picked


def forward_kernel(
    heads,
    head_dim,
    ranges,
    gates,
    q_ref,
    kv_ref,
    tkv_ref,
    meta_ref,
    mixed_ref,
    self_ref,
    cross_ref,
    lse_ref,
    max_ref,
    sum_ref,
    acc_ref,
):
    width = heads * head_dim
    rows = q_ref.shape[0]
    max_ref[...] = jnp.full(max_ref.shape, masked_score, F32)
    sum_ref[...] = jnp.zeros(sum_ref.shape, F32)
    acc_ref[...] = jnp.zeros(acc_ref.shape, F32)
    first = meta_ref[0:1, :]
    last = meta_ref[1:2, :]
    clip = meta_ref[2:3, :]

    def self_step(block, carry):
        start = pl.multiple_of(block * KEY_BLOCK, KEY_BLOCK)
        key_index = start + lax.broadcasted_iota(jnp.int32, (KEY_BLOCK, rows), 0)
        allowed = (key_index >= first) & (key_index < last)
        for h in range(heads):
            lanes = slice(h * head_dim, (h + 1) * head_dim)
            v_lanes = slice(width + h * head_dim, width + (h + 1) * head_dim)
            keys = kv_ref[pl.ds(start, KEY_BLOCK), lanes]
            values = kv_ref[pl.ds(start, KEY_BLOCK), v_lanes]
            scores = jnp.where(allowed, dot_nt(keys, q_ref[:, lanes]), masked_score)
            old_max = max_ref[h : h + 1, :]
            new_max = jnp.maximum(old_max, jnp.max(scores, 0, keepdims=True))
            probs = jnp.exp(scores - new_max)
            factor = jnp.exp(old_max - new_max)
            max_ref[h : h + 1, :] = new_max
            sum_ref[h : h + 1, :] = sum_ref[h : h + 1, :] * factor + jnp.sum(
                probs, 0, keepdims=True
            )
            acc_ref[lanes, :] = acc_ref[lanes, :] * factor + dot_tn(values, probs.astype(BF))
        return carry

    lax.fori_loop(ranges[0], ranges[1], self_step, 0)
    for h in range(heads):
        lanes = slice(h * head_dim, (h + 1) * head_dim)
        sums = sum_ref[h : h + 1, :]
        self_ref[:, lanes] = (acc_ref[lanes, :] / sums).T
        lse_ref[h : h + 1, :] = max_ref[h : h + 1, :] + jnp.log(sums)

    acc_ref[...] = jnp.zeros(acc_ref.shape, F32)

    def cross_step(which, carry):
        start = pl.multiple_of(which * CAP, CAP)
        slot = lax.broadcasted_iota(jnp.int32, (CAP, rows), 0)
        valid = slot < ranges[4 + which]
        here = clip == which
        for h in range(heads):
            lanes = slice(h * head_dim, (h + 1) * head_dim)
            v_lanes = slice(width + h * head_dim, width + (h + 1) * head_dim)
            keys = tkv_ref[pl.ds(start, CAP), lanes]
            values = tkv_ref[pl.ds(start, CAP), v_lanes]
            scores = jnp.where(valid, dot_nt(keys, q_ref[:, lanes]), masked_score)
            top = jnp.max(scores, 0, keepdims=True)
            probs = jnp.exp(scores - top)
            sums = jnp.sum(probs, 0, keepdims=True)
            probs = probs / sums
            acc_ref[lanes, :] = jnp.where(here, dot_tn(values, probs.astype(BF)), acc_ref[lanes, :])
            row = slice(heads + h, heads + h + 1)
            lse_ref[row, :] = jnp.where(here, top + jnp.log(sums), lse_ref[row, :])
        return carry

    lse_ref[heads : 2 * heads, :] = jnp.zeros((heads, rows), F32)
    lax.fori_loop(ranges[2], ranges[3], cross_step, 0)
    for h in range(heads):
        lanes = slice(h * head_dim, (h + 1) * head_dim)
        cross = acc_ref[lanes, :].T
        cross_ref[:, lanes] = cross
        mixed_ref[:, lanes] = (
            self_ref[:, lanes].astype(BF).astype(F32) + gates[h] * cross
        ).astype(BF)


def backward_kernel(
    heads,
    head_dim,
    ranges,
    gates,
    q_ref,
    kv_ref,
    tkv_ref,
    meta_ref,
    dout_ref,
    self_ref,
    lse_ref,
    dq_ref,
    dkv_ref,
    dtkv_ref,
    delta_ref,
    gated_ref,
    acc_ref,
):
    width = heads * head_dim
    rows = q_ref.shape[0]
    dkv_ref[...] = jnp.zeros(dkv_ref.shape, dkv_ref.dtype)
    dtkv_ref[...] = jnp.zeros(dtkv_ref.shape, dtkv_ref.dtype)
    acc_ref[...] = jnp.zeros(acc_ref.shape, F32)
    for h in range(heads):
        lanes = slice(h * head_dim, (h + 1) * head_dim)
        grad = dout_ref[:, lanes].astype(F32)
        delta_ref[h : h + 1, :] = jnp.sum((grad * self_ref[:, lanes]).T, 0, keepdims=True)
        gated_ref[:, lanes] = (grad * gates[h]).astype(BF)
    first = meta_ref[0:1, :]
    last = meta_ref[1:2, :]
    clip = meta_ref[2:3, :]

    def self_step(block, carry):
        start = pl.multiple_of(block * KEY_BLOCK, KEY_BLOCK)
        key_index = start + lax.broadcasted_iota(jnp.int32, (KEY_BLOCK, rows), 0)
        allowed = (key_index >= first) & (key_index < last)
        for h in range(heads):
            lanes = slice(h * head_dim, (h + 1) * head_dim)
            v_lanes = slice(width + h * head_dim, width + (h + 1) * head_dim)
            keys = kv_ref[pl.ds(start, KEY_BLOCK), lanes]
            values = kv_ref[pl.ds(start, KEY_BLOCK), v_lanes]
            queries = q_ref[:, lanes]
            grads = dout_ref[:, lanes]
            scores = dot_nt(keys, queries)
            probs = jnp.where(allowed, jnp.exp(scores - lse_ref[h : h + 1, :]), 0.0)
            prob_grad = dot_nt(values, grads)
            dkv_ref[pl.ds(start, KEY_BLOCK), v_lanes] = dot(probs.astype(BF), grads).astype(
                dkv_ref.dtype
            )
            score_grad = (probs * (prob_grad - delta_ref[h : h + 1, :])).astype(BF)
            dkv_ref[pl.ds(start, KEY_BLOCK), lanes] = dot(score_grad, queries).astype(
                dkv_ref.dtype
            )
            acc_ref[lanes, :] = acc_ref[lanes, :] + dot_tn(keys, score_grad)
        return carry

    lax.fori_loop(ranges[0], ranges[1], self_step, 0)

    def cross_step(which, carry):
        start = pl.multiple_of(which * CAP, CAP)
        slot = lax.broadcasted_iota(jnp.int32, (CAP, rows), 0)
        allowed = (slot < ranges[4 + which]) & (clip == which)
        for h in range(heads):
            lanes = slice(h * head_dim, (h + 1) * head_dim)
            v_lanes = slice(width + h * head_dim, width + (h + 1) * head_dim)
            keys = tkv_ref[pl.ds(start, CAP), lanes]
            values = tkv_ref[pl.ds(start, CAP), v_lanes]
            queries = q_ref[:, lanes]
            grads = gated_ref[:, lanes]
            scores = dot_nt(keys, queries)
            probs = jnp.where(
                allowed, jnp.exp(scores - lse_ref[heads + h : heads + h + 1, :]), 0.0
            )
            prob_grad = dot_nt(values, grads)
            dtkv_ref[pl.ds(start, CAP), v_lanes] = dot(probs.astype(BF), grads).astype(
                dtkv_ref.dtype
            )
            inner = jnp.sum(probs * prob_grad, 0, keepdims=True)
            score_grad = (probs * (prob_grad - inner)).astype(BF)
            dtkv_ref[pl.ds(start, CAP), lanes] = dot(score_grad, queries).astype(dtkv_ref.dtype)
            acc_ref[lanes, :] = acc_ref[lanes, :] + dot_tn(keys, score_grad)
        return carry

    lax.fori_loop(ranges[2], ranges[3], cross_step, 0)
    for h in range(heads):
        lanes = slice(h * head_dim, (h + 1) * head_dim)
        dq_ref[:, lanes] = acc_ref[lanes, :].T * (1.0 / math.sqrt(head_dim))


SMEM = pl.BlockSpec(memory_space=pltpu.SMEM)
WHOLE = pl.BlockSpec(memory_space=pltpu.VMEM)


def attend_forward(ranges, gates, queries, kv, tkv, meta, heads, head_dim):
    rows, width = queries.shape
    lse_rows = -(-2 * heads // 8) * 8
    work = 4 * rows * kv.shape[0] * width // 2
    return pl.pallas_call(
        functools.partial(forward_kernel, heads, head_dim),
        out_shape=(
            jax.ShapeDtypeStruct((rows, width), BF),
            jax.ShapeDtypeStruct((rows, width), F32),
            jax.ShapeDtypeStruct((rows, width), F32),
            jax.ShapeDtypeStruct((lse_rows, rows), F32),
        ),
        in_specs=[SMEM, SMEM] + [WHOLE] * 4,
        out_specs=(WHOLE,) * 4,
        scratch_shapes=[
            pltpu.VMEM((8, rows), F32),
            pltpu.VMEM((8, rows), F32),
            pltpu.VMEM((width, rows), F32),
        ],
        compiler_params=pltpu.CompilerParams(vmem_limit_bytes=VMEM_BYTES),
        cost_estimate=pl.CostEstimate(
            flops=work * 4, bytes_accessed=kv.size * 2, transcendentals=work // (4 * head_dim)
        ),
    )(ranges, gates, queries, kv, tkv, meta)


def attend_backward(ranges, gates, queries, kv, tkv, meta, dout, self_out, lse, heads, head_dim):
    rows, width = queries.shape
    work = 10 * rows * kv.shape[0] * width // 2
    return pl.pallas_call(
        functools.partial(backward_kernel, heads, head_dim),
        out_shape=(
            jax.ShapeDtypeStruct((rows, width), F32),
            jax.ShapeDtypeStruct(kv.shape, BF),
            jax.ShapeDtypeStruct(tkv.shape, BF),
        ),
        in_specs=[SMEM, SMEM] + [WHOLE] * 7,
        out_specs=(WHOLE,) * 3,
        scratch_shapes=[
            pltpu.VMEM((8, rows), F32),
            pltpu.VMEM((rows, width), BF),
            pltpu.VMEM((width, rows), F32),
        ],
        compiler_params=pltpu.CompilerParams(vmem_limit_bytes=VMEM_BYTES),
        cost_estimate=pl.CostEstimate(
            flops=work * 4, bytes_accessed=kv.size * 4, transcendentals=work // (10 * head_dim)
        ),
    )(ranges, gates, queries, kv, tkv, meta, dout, self_out, lse)


def body(
    video,
    conditioning,
    captions,
    clip_lengths,
    cap_lengths,
    positions,
    ada_weight,
    ada_bias,
    query_weight,
    key_weight,
    value_weight,
    out_weight,
    text_key_weight,
    text_value_weight,
    gate_weight,
    up_weight,
    down_weight,
    attn_gain,
    query_gain,
    key_gain,
    text_key_gain,
    attn_out_gain,
    ffn_gain,
    ffn_out_gain,
    cross_gate,
    cotangent,
):
    num_sub = lax.axis_size("sub")
    num_seq = lax.axis_size("seq")
    rows, width = video.shape
    heads_total = cross_gate.shape[0]
    head_dim = width // heads_total
    heads = heads_total // num_sub
    cols = width // num_sub
    device = lax.axis_index(BOTH)
    seq = lax.axis_index("seq")
    sub = lax.axis_index("sub")
    group = rows * num_sub
    tokens = group * num_seq
    clips = clip_lengths.shape[0]
    clip_range = jnp.arange(clips, dtype=jnp.int32)
    score_scale = 1.0 / math.sqrt(head_dim)

    ends = jnp.cumsum(clip_lengths)
    starts = ends - clip_lengths
    group_clip = clip_index(seq * group + jnp.arange(group, dtype=jnp.int32), clip_lengths)
    group_hot_bool = group_clip[:, None] == clip_range[None, :]
    group_hot = group_hot_bool.astype(F32)
    own_hot = lax.dynamic_slice_in_dim(group_hot, sub * rows, rows, 0)
    first = jnp.sum(jnp.where(group_hot_bool, starts[None, :], 0), 1)
    last = jnp.sum(jnp.where(group_hot_bool, ends[None, :], 0), 1)
    meta = jnp.concatenate(
        [first[None], last[None], group_clip[None], jnp.zeros((5, group), jnp.int32)], 0
    )
    ranges = jnp.concatenate(
        [
            jnp.stack(
                [
                    first[0] // KEY_BLOCK,
                    (last[-1] + KEY_BLOCK - 1) // KEY_BLOCK,
                    group_clip[0],
                    group_clip[-1] + 1,
                ]
            ),
            cap_lengths,
        ]
    ).astype(jnp.int32)
    gate_tanh = jnp.tanh(cross_gate.astype(F32))
    gates = lax.dynamic_slice_in_dim(gate_tanh, sub * heads, heads, 0)

    cond_float = conditioning.astype(F32)
    cond_act = jax.nn.silu(cond_float).astype(BF)
    cond_rows = ada_weight.shape[0]
    cond_slice = lax.dynamic_slice_in_dim(cond_act, device * cond_rows, cond_rows, 1)
    mod_part = dot(cond_slice, ada_weight)
    mod_part = mod_part + lax.dynamic_update_slice_in_dim(
        jnp.zeros((1, 4 * width), F32), ada_bias.astype(F32)[None], device * ada_bias.shape[0], 1
    )
    mod_part = mod_part.reshape(clips, 4, width)
    gain_rows = attn_gain.shape[0]

    def spread(gains):
        stacked = jnp.stack(gains).astype(F32)
        return lax.dynamic_update_slice_in_dim(
            jnp.zeros((len(gains), width), F32), stacked, device * gain_rows, 1
        )

    early = total(
        jnp.concatenate([mod_part[:, 0], spread([attn_gain, query_gain, key_gain])], 0),
        ("sub", "seq"),
    )
    late = total(
        jnp.concatenate(
            [
                mod_part[:, 1],
                mod_part[:, 2],
                mod_part[:, 3],
                spread([text_key_gain, attn_out_gain, ffn_gain, ffn_out_gain]),
            ],
            0,
        ),
        ("sub", "seq"),
    )
    scale_rows = early[:clips]
    attn_gain_f = early[clips : clips + 1]
    query_gain_f = lax.dynamic_slice_in_dim(early[clips + 1 : clips + 2], sub * cols, cols, 1)
    key_gain_f = lax.dynamic_slice_in_dim(early[clips + 2 : clips + 3], sub * cols, cols, 1)
    attn_gate = pick_rows(own_hot, late[:clips])
    ffn_scale = pick_rows(own_hot, late[clips : 2 * clips])
    ffn_gate = pick_rows(own_hot, late[2 * clips : 3 * clips])
    text_key_gain_f = lax.dynamic_slice_in_dim(
        late[3 * clips : 3 * clips + 1], sub * cols, cols, 1
    )
    attn_out_f = late[3 * clips + 1 : 3 * clips + 2]
    ffn_gain_f = late[3 * clips + 2 : 3 * clips + 3]
    ffn_out_f = late[3 * clips + 3 : 3 * clips + 4]

    packed = jnp.concatenate(
        [video, jnp.pad(positions.astype(BF), ((0, 0), (0, 128 - positions.shape[1])))], 1
    )
    packed = gather_line(packed, "sub")
    video_group = packed[:, :width].astype(F32)
    group_pos = packed[:, width : width + 3].astype(F32)
    w_rows = query_weight.shape[0]
    qkv_weight = jnp.concatenate(
        [w.reshape(w_rows, num_sub, cols) for w in (query_weight, key_weight, value_weight)], 2
    ).transpose(1, 0, 2)
    qkv_weight = swap_blocks(qkv_weight, "sub").reshape(num_sub * w_rows, 3 * cols)
    qkv_weight = gather_rows(qkv_weight, "seq")

    cap_shard = captions.shape[0]
    cap_total = cap_shard * num_sub
    t_rows = text_key_weight.shape[0]
    cap_cols = lax.dynamic_slice_in_dim(
        captions, seq * num_sub * t_rows, num_sub * t_rows, 1
    ).reshape(cap_shard, num_sub, t_rows)
    cap_cols = swap_blocks(cap_cols.transpose(1, 0, 2), "sub").reshape(cap_total, t_rows)
    text_weight = jnp.concatenate(
        [
            text_key_weight.reshape(t_rows, num_sub, 1, cols),
            text_value_weight.reshape(t_rows, num_sub, 1, cols),
        ],
        2,
    ).reshape(t_rows, 2 * width)
    text_part = dot(cap_cols, text_weight).astype(BF)
    text_part = scatter_rows(text_part, "seq")
    slots = cap_total // num_seq
    text_part = text_part.reshape(slots, num_sub, 2 * cols).transpose(1, 0, 2)
    text_pre = jnp.sum(swap_blocks(text_part, "sub").astype(F32), 0)
    text_key_pre = text_pre[:, :cols]
    text_square = total(jnp.sum(text_key_pre * text_key_pre, 1)[None], ("sub",))
    text_inv = lax.rsqrt(text_square / width + epsilon).reshape(slots, 1)
    text_hat = text_key_pre * text_inv
    tkv = jnp.concatenate(
        [(text_hat * text_key_gain_f).astype(BF), text_pre[:, cols:].astype(BF)], 1
    )
    tkv = gather_rows(tkv, "seq")

    out_full = gather_rows(out_weight, BOTH)
    units = gate_weight.shape[1] // num_seq
    gate_up = jnp.concatenate(
        [w.reshape(w_rows, num_seq, units) for w in (gate_weight, up_weight)], 2
    ).transpose(1, 0, 2)
    gate_up = swap_blocks(gate_up, "seq").reshape(num_seq * w_rows, 2 * units)
    gate_up = gather_rows(gate_up, "sub")
    gate_up = (
        gate_up.reshape(num_sub, num_seq, w_rows, 2 * units)
        .transpose(1, 0, 2, 3)
        .reshape(width, 2 * units)
    )
    down_block = gather_rows(down_weight, "sub")

    video_inv = inv_rms(video_group)
    video_hat = video_group * video_inv
    attn_scale1 = 1.0 + pick_rows(group_hot, scale_rows)
    normed = (video_hat * (attn_gain_f * attn_scale1)).astype(BF)
    qkv_pre = dot(normed, qkv_weight)
    query_pre = qkv_pre[:, :cols]
    key_pre = qkv_pre[:, cols : 2 * cols]
    squares = total(
        jnp.stack([jnp.sum(query_pre * query_pre, 1), jnp.sum(key_pre * key_pre, 1)]), ("sub",)
    )
    inverse = lax.rsqrt(squares / width + epsilon)
    query_inv = inverse[0].reshape(group, 1)
    key_inv = inverse[1].reshape(group, 1)
    query_hat = query_pre * query_inv
    key_hat = key_pre * key_inv
    cosine, sine = rope_tables(group_pos, head_dim, heads)
    queries = (rotate(query_hat * query_gain_f, cosine, sine).astype(BF) * score_scale).astype(BF)
    keys = rotate(key_hat * key_gain_f, cosine, sine).astype(BF)
    kv = gather_rows(jnp.concatenate([keys, qkv_pre[:, 2 * cols :].astype(BF)], 1), "seq")

    mixed_heads, self_out, cross_out, lse = attend_forward(
        ranges, gates, queries, kv, tkv, meta, heads, head_dim
    )
    mixed = (
        swap_blocks(mixed_heads.reshape(num_sub, rows, cols), "sub")
        .transpose(1, 0, 2)
        .reshape(rows, width)
    )

    video_own = video.astype(F32)
    projected = dot(mixed, out_full)
    proj_inv = inv_rms(projected)
    proj_hat = projected * proj_inv
    attn_tanh = jnp.tanh(attn_gate)
    hidden_state = video_own + attn_tanh * proj_hat * attn_out_f
    hidden_inv = inv_rms(hidden_state)
    hidden_hat = hidden_state * hidden_inv
    ffn_mult = ffn_gain_f * (1.0 + ffn_scale)
    ffn_in = gather_seq((hidden_hat * ffn_mult).astype(BF))
    gate_up_pre = dot(ffn_in, gate_up)
    gate_pre = gate_up_pre[:, :units]
    up_pre = gate_up_pre[:, units:]
    gate_sig = jax.nn.sigmoid(gate_pre)
    gate_act = gate_pre * gate_sig
    activated = (gate_act * up_pre).astype(BF)
    down_out = scatter_seq(dot(activated, down_block).astype(BF)).astype(F32)
    down_inv = inv_rms(down_out)
    down_hat = down_out * down_inv
    ffn_tanh = jnp.tanh(ffn_gate)
    block_out = (hidden_state + ffn_tanh * down_hat * ffn_out_f).astype(BF)

    grad_out = cotangent.astype(F32)
    ffn_gate_grad = grad_out * down_hat * ffn_out_f * (1.0 - ffn_tanh * ffn_tanh)
    ffn_out_gain_part = jnp.sum(grad_out * ffn_tanh * down_hat, 0)
    down_grad = gather_seq(
        norm_back(down_hat, down_inv, grad_out * ffn_tanh * ffn_out_f).astype(BF)
    )
    down_weight_term = dot_tn(activated, down_grad).astype(BF)
    act_grad = dot_nt(down_grad, down_block)
    gate_grad = (act_grad * up_pre * gate_sig * (1.0 + gate_pre * (1.0 - gate_sig))).astype(BF)
    up_grad = (act_grad * gate_act).astype(BF)
    gate_up_grad = jnp.concatenate([gate_grad, up_grad], 1)
    ffn_in_grad = scatter_seq(dot_nt(gate_up_grad, gate_up).astype(BF)).astype(F32)
    gate_up_term = dot_tn(ffn_in, gate_up_grad).astype(BF)
    down_weight_grad = scatter_rows(down_weight_term, "sub").astype(F32)
    gate_up_term = (
        gate_up_term.reshape(num_seq, num_sub, w_rows, 2 * units)
        .transpose(1, 0, 2, 3)
        .reshape(width, 2 * units)
    )
    gate_up_term = scatter_rows(gate_up_term, "sub").reshape(num_seq, w_rows, 2 * units)
    gate_up_term = swap_blocks(gate_up_term, "seq").transpose(1, 0, 2).astype(F32)
    gate_weight_grad = gate_up_term[:, :, :units].reshape(w_rows, num_seq * units)
    up_weight_grad = gate_up_term[:, :, units:].reshape(w_rows, num_seq * units)

    ffn_gain_part = jnp.sum(ffn_in_grad * hidden_hat * (1.0 + ffn_scale), 0)
    ffn_scale_grad = ffn_in_grad * hidden_hat * ffn_gain_f
    hidden_grad = grad_out + norm_back(hidden_hat, hidden_inv, ffn_in_grad * ffn_mult)
    attn_gate_grad = hidden_grad * proj_hat * attn_out_f * (1.0 - attn_tanh * attn_tanh)
    attn_out_gain_part = jnp.sum(hidden_grad * attn_tanh * proj_hat, 0)
    proj_grad = norm_back(proj_hat, proj_inv, hidden_grad * attn_tanh * attn_out_f).astype(BF)
    mixed_grad = dot_nt(proj_grad, out_full).astype(BF)
    out_weight_term = dot_tn(mixed, proj_grad).astype(BF)
    out_weight_grad = scatter_rows(scatter_rows(out_weight_term, "seq"), "sub").astype(F32)

    dout = swap_blocks(
        mixed_grad.reshape(rows, num_sub, cols).transpose(1, 0, 2), "sub"
    ).reshape(group, cols)
    cross_gate_part = jnp.sum(
        (dout.astype(F32) * cross_out).reshape(group, heads, head_dim), (0, 2)
    ) * (1.0 - gates * gates)
    query_rot_grad, dkv, dtkv = attend_backward(
        ranges, gates, queries, kv, tkv, meta, dout, self_out, lse, heads, head_dim
    )
    query_rot_grad = query_rot_grad.astype(BF).astype(F32)
    dkv = scatter_seq(dkv)
    key_rot_grad = dkv[:, :cols].astype(F32)
    value_grad = dkv[:, cols:]
    query_norm_grad = rotate(query_rot_grad, cosine, -sine)
    query_gain_part = jnp.sum(query_norm_grad * query_hat, 0)
    query_hat_grad = query_norm_grad * query_gain_f
    key_norm_grad = rotate(key_rot_grad, cosine, -sine)
    key_gain_part = jnp.sum(key_norm_grad * key_hat, 0)
    key_hat_grad = key_norm_grad * key_gain_f
    inner = total(
        jnp.stack([jnp.sum(query_hat * query_hat_grad, 1), jnp.sum(key_hat * key_hat_grad, 1)]),
        ("sub",),
    ) / width
    query_pre_grad = query_inv * (query_hat_grad - query_hat * inner[0].reshape(group, 1))
    key_pre_grad = key_inv * (key_hat_grad - key_hat * inner[1].reshape(group, 1))
    qkv_grad = jnp.concatenate([query_pre_grad.astype(BF), key_pre_grad.astype(BF), value_grad], 1)
    qkv_term = dot_tn(normed, qkv_grad).astype(BF)
    normed_part = dot_nt(qkv_grad, qkv_weight)
    normed_grad = scatter_rows(normed_part.astype(BF), "sub").astype(F32)
    qkv_term = scatter_seq(qkv_term).reshape(num_sub, w_rows, 3 * cols)
    qkv_term = swap_blocks(qkv_term, "sub").transpose(1, 0, 2).astype(F32)
    query_weight_grad, key_weight_grad, value_weight_grad = (
        qkv_term[:, :, i * cols : (i + 1) * cols].reshape(w_rows, width) for i in range(3)
    )

    own_hat = lax.dynamic_slice_in_dim(video_hat, sub * rows, rows, 0)
    own_inv = lax.dynamic_slice_in_dim(video_inv, sub * rows, rows, 0)
    own_scale1 = lax.dynamic_slice_in_dim(attn_scale1, sub * rows, rows, 0)
    video_grad = hidden_grad + norm_back(own_hat, own_inv, normed_grad * (attn_gain_f * own_scale1))
    hat_grad = normed_part * video_hat
    attn_gain_part = jnp.sum(hat_grad * attn_scale1, 0)
    scale_part = dot_tn(group_hot.astype(BF), (hat_grad * attn_gain_f).astype(BF))

    dtkv = scatter_rows(dtkv, "seq")
    text_key_low = dtkv[:, :cols].astype(F32)
    text_key_gain_part = jnp.sum(text_key_low * text_hat, 0)
    text_hat_grad = text_key_low * text_key_gain_f
    text_inner = total(jnp.sum(text_hat * text_hat_grad, 1)[None], ("sub",)) / width
    text_pre_grad = text_inv * (text_hat_grad - text_hat * text_inner.reshape(slots, 1))
    text_grad = jnp.concatenate([text_pre_grad.astype(BF), dtkv[:, cols:]], 1)
    text_grad = gather_rows(text_grad, BOTH)
    text_grad = (
        text_grad.reshape(num_seq, num_sub, slots, 2 * cols)
        .transpose(0, 2, 1, 3)
        .reshape(cap_total, 2 * width)
    )
    text_term = dot_tn(cap_cols, text_grad).reshape(t_rows, num_sub, 2, cols)
    text_key_weight_grad = text_term[:, :, 0].reshape(t_rows, width)
    text_value_weight_grad = text_term[:, :, 1].reshape(t_rows, width)
    caption_cols = dot_nt(text_grad, text_weight).astype(BF).reshape(num_sub, cap_shard, t_rows)
    caption_cols = (
        swap_blocks(caption_cols, "sub").transpose(1, 0, 2).reshape(cap_shard, num_sub * t_rows)
    )
    caption_grad = (
        gather_rows(caption_cols[None], "seq")
        .transpose(1, 0, 2)
        .reshape(cap_shard, captions.shape[1])
        .astype(F32)
    )

    def clip_sums(values):
        return dot_tn(own_hot.astype(BF), values.astype(BF))

    def place(part):
        return lax.dynamic_update_slice_in_dim(
            jnp.zeros((1, width), F32), part.reshape(1, -1), sub * cols, 1
        )

    gate_row = lax.dynamic_update_slice_in_dim(
        jnp.zeros((1, width), F32), cross_gate_part.reshape(1, -1), sub * heads, 1
    )
    late_sum = total(
        jnp.concatenate(
            [
                clip_sums(attn_gate_grad),
                clip_sums(ffn_scale_grad),
                clip_sums(ffn_gate_grad),
                attn_out_gain_part[None],
                ffn_gain_part[None],
                ffn_out_gain_part[None],
                gate_row,
            ],
            0,
        ),
        ("sub", "seq"),
    )
    early_sum = total(
        jnp.concatenate(
            [
                scale_part,
                attn_gain_part[None],
                place(query_gain_part),
                place(key_gain_part),
                place(text_key_gain_part),
            ],
            0,
        ),
        ("sub", "seq"),
    )

    def own_gain(row):
        return lax.dynamic_slice_in_dim(row, device * gain_rows, gain_rows, 0)

    mod_low = jnp.concatenate(
        [
            early_sum[:clips],
            late_sum[:clips],
            late_sum[clips : 2 * clips],
            late_sum[2 * clips : 3 * clips],
        ],
        1,
    ).astype(BF)
    bias_rows = ada_bias.shape[0]
    ada_bias_grad = jnp.sum(
        lax.dynamic_slice_in_dim(mod_low.astype(F32), device * bias_rows, bias_rows, 1), 0
    )
    ada_weight_grad = dot_tn(cond_slice, mod_low)
    cond_part = lax.dynamic_update_slice_in_dim(
        jnp.zeros(conditioning.shape, F32), dot_nt(mod_low, ada_weight), device * cond_rows, 1
    )
    cond_sig = jax.nn.sigmoid(cond_float)
    cond_grad = (
        total(cond_part, ("sub", "seq")) * cond_sig * (1.0 + cond_float * (1.0 - cond_sig))
    )
    return (
        block_out,
        video_grad,
        caption_grad,
        cond_grad,
        ada_weight_grad,
        ada_bias_grad,
        query_weight_grad,
        key_weight_grad,
        value_weight_grad,
        out_weight_grad,
        text_key_weight_grad,
        text_value_weight_grad,
        gate_weight_grad,
        up_weight_grad,
        down_weight_grad,
        own_gain(early_sum[clips]),
        own_gain(early_sum[clips + 1]),
        own_gain(early_sum[clips + 2]),
        own_gain(early_sum[clips + 3]),
        own_gain(late_sum[3 * clips]),
        own_gain(late_sum[3 * clips + 1]),
        own_gain(late_sum[3 * clips + 2]),
        late_sum[3 * clips + 3, :heads_total],
    )


def solution(mesh):
    matrix = P(BOTH, None)
    vector = P(BOTH)
    return jax.shard_map(
        body,
        mesh=mesh,
        in_specs=(matrix, P(), P("sub", None), P(), P(), matrix, matrix, vector)
        + (matrix,) * 9
        + (vector,) * 7
        + (P(), matrix),
        out_specs=(matrix, matrix, P("sub", None), P(), matrix, vector)
        + (matrix,) * 9
        + (vector,) * 7
        + (P(),),
        check_vma=False,
    )
```

```python
import functools
import math

import jax
import jax.numpy as jnp
import numpy as np
from jax import lax
from jax.experimental import pallas as pl
from jax.experimental.pallas import tpu as pltpu
from jax.sharding import PartitionSpec as P

CAP = 256
KEY_BLOCK = 512
epsilon = 1e-06
rope_base = 10000.0
masked_score = -1e30
BF = jnp.bfloat16
F32 = jnp.float32
BOTH = ("seq", "sub")
VMEM_BYTES = 56 * 1024 * 1024
KERNEL_WORK = 16


def axis_bits(axis):
    masks, mask = [], 1
    while mask < lax.axis_size(axis):
        masks.append(mask)
        mask *= 2
    return masks


def send(values, axis, mask):
    count = lax.axis_size(axis)
    return lax.ppermute(values, axis, [(i, i ^ mask) for i in range(count)])


class Flow:
    def __init__(self, stages):
        self.stages = stages
        self.result = None
        self.done = False
        self.wanted = next(stages)

    def feed(self, arrived):
        try:
            self.wanted = self.stages.send(arrived)
        except StopIteration as stop:
            self.wanted, self.done, self.result = [], True, stop.value


class Schedule:
    def __init__(self):
        self.frontier = ()

    def tie(self, *arrays):
        tied = lax.optimization_barrier(tuple(arrays) + self.frontier)
        return tied[: len(arrays)]

    def step(self, *flows, work=None, args=()):
        flows = [flow for flow in flows if not flow.done]
        sends = [item for flow in flows for item in flow.wanted]
        tied = self.tie(*[item[0] for item in sends], *args)
        arrived = [send(value, item[1], item[2]) for value, item in zip(tied, sends)]
        outputs = work(*tied[len(sends) :]) if work is not None else ()
        self.frontier = tuple(arrived) + tuple(jax.tree.leaves(outputs))
        for flow in flows:
            count = len(flow.wanted)
            flow.feed(arrived[:count])
            arrived = arrived[count:]
        return outputs

    def start(self, flow, *others):
        tied = lax.optimization_barrier(
            tuple(item[0] for item in flow.wanted) + self.frontier + tuple(others)
        )
        flow.feed([send(v, item[1], item[2]) for v, item in zip(tied, flow.wanted)])
        return flow.result

    def held(self, values):
        return list(self.tie(*values))


def in_order(pieces, index):
    mask = 1
    while mask < len(pieces):
        flip = (index // mask) % 2 == 1
        pieces = [jnp.where(flip, pieces[i ^ mask], pieces[i]) for i in range(len(pieces))]
        mask *= 2
    return pieces


def rows_in_order(pieces, index):
    shape = pieces[0][1].shape
    result = jnp.zeros((len(pieces),) + shape, pieces[0][1].dtype)
    for mask, piece in pieces:
        result = lax.dynamic_update_index_in_dim(result, piece, index ^ mask, 0)
    return result.reshape((len(pieces) * shape[0],) + shape[1:])


def gather_even_odd(values, axis="seq"):
    arrived = yield [(values, axis, mask) for mask in range(2, lax.axis_size(axis), 2)]
    even = jnp.concatenate([values] + arrived, 0)
    (odd,) = yield [(even, axis, 1)]
    return even, odd


def scatter_even_odd(even, odd, axis="seq"):
    count = lax.axis_size(axis) // 2
    rows = even.shape[0] // count
    (other,) = yield [(odd, axis, 1)]
    held = (even.astype(F32) + other.astype(F32)).astype(even.dtype)
    arrived = yield [
        (held[i * rows : (i + 1) * rows], axis, 2 * i) for i in range(1, count)
    ]
    result = held[:rows].astype(F32)
    for piece in arrived:
        result = result + piece.astype(F32)
    return result


def gather_seq(values, dim=0, dtype=None):
    even, odd = yield from gather_even_odd(values)
    return place(even, odd, lax.axis_index("seq"), dim, dtype or values.dtype)


def scatter_seq(values):
    index = lax.axis_index("seq")
    count = lax.axis_size("seq")
    blocks = values.reshape((count, values.shape[0] // count) + values.shape[1:])
    halves = [
        jnp.concatenate(
            [
                lax.dynamic_index_in_dim(blocks, index ^ mask, 0, keepdims=False)
                for mask in range(core, count, 2)
            ],
            0,
        )
        for core in range(2)
    ]
    result = yield from scatter_even_odd(*halves)
    return result


def pair_sum(pieces):
    while len(pieces) > 1:
        pieces = [pieces[i] + pieces[i + 1] for i in range(0, len(pieces), 2)]
    return pieces[0]


def total(values, axes):
    for axis in axes:
        groups = [range(1, lax.axis_size(axis))]
        if axis == "seq":
            groups = [range(2, lax.axis_size(axis), 2), [1]]
        for masks in groups:
            arrived = yield [(values, axis, mask) for mask in masks]
            values = pair_sum([values] + arrived)
    return values


def total_cube(values, axes):
    for axis in axes:
        for mask in axis_bits(axis):
            (other,) = yield [(values, axis, mask)]
            values = values + other
    return values


def total_rows(values, axis="sub"):
    count = lax.axis_size(axis)
    rows = values.shape[1] // count
    arrived = yield [(values, axis, mask) for mask in range(1, count)]
    for mask, other in enumerate(arrived, 1):
        values = values + jnp.concatenate(
            [other[:, (i ^ mask) * rows : ((i ^ mask) + 1) * rows] for i in range(count)], 1
        )
    return values


def gather_direct(values, axis="sub"):
    arrived = yield [(values, axis, mask) for mask in range(1, lax.axis_size(axis))]
    return [values] + arrived


def swap_direct(blocks, axis="sub"):
    arrived = yield [(blocks[mask], axis, mask) for mask in range(1, len(blocks))]
    return [blocks[0]] + arrived


def scatter_direct(blocks, axis="sub"):
    arrived = yield [(blocks[mask], axis, mask) for mask in range(1, len(blocks))]
    result = blocks[0].astype(F32)
    for other in arrived:
        result = result + other.astype(F32)
    return result


def blocks_for(values, dim, axis="sub"):
    index = lax.axis_index(axis)
    count = lax.axis_size(axis)
    size = values.shape[dim] // count
    if dim == 0:
        blocks = values.reshape((count, size) + values.shape[1:])
        return [
            lax.dynamic_index_in_dim(blocks, index ^ mask, 0, keepdims=False)
            for mask in range(count)
        ]
    return in_order([values[:, i * size : (i + 1) * size] for i in range(count)], index)


def swap_blocks(values, axis):
    return lax.all_to_all(values, axis, split_axis=0, concat_axis=0, tiled=True)


def swap_copies(values, axis="sub"):
    return swap_blocks(jnp.broadcast_to(values[None], (lax.axis_size(axis),) + values.shape), axis)


def gather_rows(values, axis):
    return lax.all_gather(values, axis, axis=0, tiled=True)


def scatter_rows(values, axis):
    return lax.psum_scatter(values, axis, scatter_dimension=0, tiled=True)


def inv_rms(values):
    return lax.rsqrt(jnp.mean(values * values, -1, keepdims=True) + epsilon)


def norm_back(normed_hat, inverse, grad_hat):
    return inverse * (grad_hat - normed_hat * jnp.mean(normed_hat * grad_hat, -1, keepdims=True))


def dot(left, right):
    return jnp.dot(left, right, preferred_element_type=F32)


def dot_nt(left, right):
    return lax.dot_general(left, right, (((1,), (1,)), ((), ())), preferred_element_type=F32)


def dot_tn(left, right):
    return lax.dot_general(left, right, (((0,), (0,)), ((), ())), preferred_element_type=F32)


def rope_tables(positions, head_dim, heads):
    pair_total = head_dim // 2
    frame_pairs = pair_total // 4
    height_pairs = (pair_total - frame_pairs) // 2
    width_pairs = pair_total - frame_pairs - height_pairs
    frequency = np.zeros((3, pair_total), np.float32)
    start = 0
    for axis_id, pair_count in enumerate((frame_pairs, height_pairs, width_pairs)):
        exponent = -np.arange(pair_count, dtype=np.float32) / np.float32(pair_count)
        frequency[axis_id, start : start + pair_count] = np.float32(rope_base) ** exponent
        start += pair_count
    frequency = jnp.asarray(np.repeat(frequency, 2, axis=1))
    angles = (
        positions[:, 0:1] * frequency[0:1]
        + positions[:, 1:2] * frequency[1:2]
        + positions[:, 2:3] * frequency[2:3]
    )
    sign = jnp.asarray(np.where(np.arange(head_dim) % 2 == 0, -1.0, 1.0).astype(np.float32))
    cosine = jnp.cos(angles)
    sine = jnp.sin(angles) * sign[None, :]
    return (jnp.tile(cosine, (1, heads)), jnp.tile(sine, (1, heads)))


def rotate(values, cosine, sine):
    even = lax.broadcasted_iota(jnp.int32, values.shape, 1) % 2 == 0
    swapped = jnp.where(even, jnp.roll(values, -1, 1), jnp.roll(values, 1, 1))
    return values * cosine + swapped * sine


def clip_index(token_index, clip_lengths):
    bounds = jnp.cumsum(clip_lengths)
    return jnp.sum((token_index[:, None] >= bounds[None, :]).astype(jnp.int32), 1)


def pick_rows(onehot, rows):
    picked = onehot[:, 0:1] * rows[0:1]
    for clip in range(1, rows.shape[0]):
        picked = picked + onehot[:, clip : clip + 1] * rows[clip : clip + 1]
    return picked


def own_lanes(block, head, head_dim):
    if block.shape[1] == head_dim:
        return block
    lane = lax.broadcasted_iota(jnp.int32, block.shape, 1)
    return jnp.where(lane // head_dim == head, block, jnp.zeros_like(block))


def key_blocks(ranges, own_rows, rows, visit):
    per_group = rows // KEY_BLOCK
    per_block = KEY_BLOCK // own_rows

    def step(place, carry):
        block = (place // per_group) * per_group
        block = block + ((place % per_group) ^ (ranges[5] // per_block))
        row = lax.broadcasted_iota(jnp.int32, (KEY_BLOCK, rows), 0)
        index = place * KEY_BLOCK + (row ^ ((ranges[5] % per_block) * own_rows))
        visit(pl.multiple_of(block * KEY_BLOCK, KEY_BLOCK), index)
        return carry

    lax.fori_loop(ranges[0], ranges[1], step, 0)


def self_forward_kernel(
    head_dim,
    lanes,
    own_rows,
    ranges,
    q_ref,
    kv_ref,
    meta_ref,
    self_ref,
    lse_ref,
    max_ref,
    sum_ref,
    acc_ref,
):
    rows, width = q_ref.shape
    per = lanes // head_dim
    max_ref[...] = jnp.full(max_ref.shape, masked_score, F32)
    sum_ref[...] = jnp.zeros(sum_ref.shape, F32)
    acc_ref[...] = jnp.zeros(acc_ref.shape, F32)
    first = meta_ref[0:1, :]
    last = meta_ref[1:2, :]

    def visit(start, key_index):
        allowed = (key_index >= first) & (key_index < last)
        for part in range(width // lanes):
            k_lanes = slice(part * lanes, (part + 1) * lanes)
            keys = kv_ref[pl.ds(start, KEY_BLOCK), k_lanes]
            values = kv_ref[pl.ds(start, KEY_BLOCK), width + part * lanes : width + (part + 1) * lanes]
            for j in range(per):
                h = part * per + j
                own = slice(h * head_dim, (h + 1) * head_dim)
                queries = own_lanes(q_ref[:, k_lanes], j, head_dim)
                scores = jnp.where(allowed, dot_nt(keys, queries), masked_score)
                old_max = max_ref[h : h + 1, :]
                new_max = jnp.maximum(old_max, jnp.max(scores, 0, keepdims=True))
                probs = jnp.exp(scores - new_max)
                factor = jnp.exp(old_max - new_max)
                max_ref[h : h + 1, :] = new_max
                sum_ref[h : h + 1, :] = sum_ref[h : h + 1, :] * factor + jnp.sum(
                    probs, 0, keepdims=True
                )
                product = dot_tn(values, probs.astype(BF))[j * head_dim : (j + 1) * head_dim, :]
                acc_ref[own, :] = acc_ref[own, :] * factor + product

    key_blocks(ranges, own_rows, rows, visit)
    lse_ref[...] = jnp.zeros(lse_ref.shape, F32)
    for h in range(width // head_dim):
        own = slice(h * head_dim, (h + 1) * head_dim)
        sums = sum_ref[h : h + 1, :]
        acc_ref[own, :] = acc_ref[own, :] / sums
        lse_ref[h : h + 1, :] = max_ref[h : h + 1, :] + jnp.log(sums)
    for part in range(width // lanes):
        own = slice(part * lanes, (part + 1) * lanes)
        self_ref[:, own] = acc_ref[own, :].T


def cross_forward_kernel(
    head_dim, lanes, ranges, gates, q_ref, tkv_ref, meta_ref, self_ref, mixed_ref, cross_ref, lse_ref, acc_ref
):
    rows, width = q_ref.shape
    acc_ref[...] = jnp.zeros(acc_ref.shape, F32)
    lse_ref[...] = jnp.zeros(lse_ref.shape, F32)
    clip = meta_ref[2:3, :]
    per = lanes // head_dim

    def step(which, carry):
        start = pl.multiple_of(which * CAP, CAP)
        slot = lax.broadcasted_iota(jnp.int32, (CAP, rows), 0)
        valid = slot < ranges[6 + which]
        here = clip == which
        for part in range(width // lanes):
            keys = tkv_ref[pl.ds(start, CAP), part * lanes : (part + 1) * lanes]
            values = tkv_ref[pl.ds(start, CAP), width + part * lanes : width + (part + 1) * lanes]
            queries = q_ref[:, part * lanes : (part + 1) * lanes]
            for j in range(per):
                h = part * per + j
                own = slice(h * head_dim, (h + 1) * head_dim)
                scores = dot_nt(keys, own_lanes(queries, j, head_dim))
                scores = jnp.where(valid, scores, masked_score)
                top = jnp.max(scores, 0, keepdims=True)
                probs = jnp.exp(scores - top)
                sums = jnp.sum(probs, 0, keepdims=True)
                probs = (probs / sums).astype(BF)
                product = dot_tn(values, probs)[j * head_dim : (j + 1) * head_dim, :]
                acc_ref[own, :] = jnp.where(here, product, acc_ref[own, :])
                lse_ref[h : h + 1, :] = jnp.where(here, top + jnp.log(sums), lse_ref[h : h + 1, :])
        return carry

    lax.fori_loop(ranges[2], ranges[3], step, 0)
    lane = lax.broadcasted_iota(jnp.int32, (1, lanes), 1)
    for part in range(width // lanes):
        own = slice(part * lanes, (part + 1) * lanes)
        cross = acc_ref[own, :].T
        gate = jnp.full((1, lanes), gates[part * per], F32)
        for j in range(1, per):
            gate = jnp.where(lane // head_dim == j, gates[part * per + j], gate)
        cross_ref[:, own] = cross
        mixed_ref[:, own] = (self_ref[:, own].astype(BF).astype(F32) + gate * cross).astype(BF)


def cross_backward_kernel(
    head_dim, lanes, ranges, gates, q_ref, tkv_ref, meta_ref, dout_ref, lse_ref, acc_ref, dtkv_ref, gated_ref
):
    rows, width = q_ref.shape
    per = lanes // head_dim
    dtkv_ref[...] = jnp.zeros(dtkv_ref.shape, dtkv_ref.dtype)
    acc_ref[...] = jnp.zeros(acc_ref.shape, F32)
    lane = lax.broadcasted_iota(jnp.int32, (1, lanes), 1)
    for part in range(width // lanes):
        own = slice(part * lanes, (part + 1) * lanes)
        gate = jnp.full((1, lanes), gates[part * per], F32)
        for j in range(1, per):
            gate = jnp.where(lane // head_dim == j, gates[part * per + j], gate)
        gated_ref[:, own] = (dout_ref[:, own].astype(F32) * gate).astype(BF)
    clip = meta_ref[2:3, :]

    def step(which, carry):
        start = pl.multiple_of(which * CAP, CAP)
        slot = lax.broadcasted_iota(jnp.int32, (CAP, rows), 0)
        allowed = (slot < ranges[6 + which]) & (clip == which)
        for part in range(width // lanes):
            k_lanes = slice(part * lanes, (part + 1) * lanes)
            v_lanes = slice(width + part * lanes, width + (part + 1) * lanes)
            keys = tkv_ref[pl.ds(start, CAP), k_lanes]
            values = tkv_ref[pl.ds(start, CAP), v_lanes]
            key_grad = value_grad = 0.0
            for j in range(per):
                h = part * per + j
                own = slice(h * head_dim, (h + 1) * head_dim)
                queries = own_lanes(q_ref[:, k_lanes], j, head_dim)
                grads = own_lanes(gated_ref[:, k_lanes], j, head_dim)
                scores = dot_nt(keys, queries)
                probs = jnp.where(allowed, jnp.exp(scores - lse_ref[h : h + 1, :]), 0.0)
                prob_grad = dot_nt(values, grads)
                value_grad = value_grad + dot(probs.astype(BF), grads)
                inner = jnp.sum(probs * prob_grad, 0, keepdims=True)
                score_grad = (probs * (prob_grad - inner)).astype(BF)
                key_grad = key_grad + dot(score_grad, queries)
                product = dot_tn(keys, score_grad)[j * head_dim : (j + 1) * head_dim, :]
                acc_ref[own, :] = acc_ref[own, :] + product
            dtkv_ref[pl.ds(start, CAP), k_lanes] = key_grad.astype(dtkv_ref.dtype)
            dtkv_ref[pl.ds(start, CAP), v_lanes] = value_grad.astype(dtkv_ref.dtype)
        return carry

    lax.fori_loop(ranges[2], ranges[3], step, 0)


def self_backward_kernel(
    head_dim,
    lanes,
    own_rows,
    ranges,
    q_ref,
    kv_ref,
    meta_ref,
    dout_ref,
    self_ref,
    lse_ref,
    start_ref,
    dq_ref,
    dkv_ref,
    delta_ref,
    acc_ref,
):
    rows, width = q_ref.shape
    per = lanes // head_dim
    dkv_ref[...] = jnp.zeros(dkv_ref.shape, dkv_ref.dtype)
    acc_ref[...] = start_ref[...]
    for part in range(width // lanes):
        own = slice(part * lanes, (part + 1) * lanes)
        product = (dout_ref[:, own].astype(F32) * self_ref[:, own]).T
        for j in range(per):
            h = part * per + j
            delta_ref[h : h + 1, :] = jnp.sum(
                product[j * head_dim : (j + 1) * head_dim, :], 0, keepdims=True
            )
    first = meta_ref[0:1, :]
    last = meta_ref[1:2, :]

    def visit(start, key_index):
        allowed = (key_index >= first) & (key_index < last)
        for part in range(width // lanes):
            k_lanes = slice(part * lanes, (part + 1) * lanes)
            v_lanes = slice(width + part * lanes, width + (part + 1) * lanes)
            keys = kv_ref[pl.ds(start, KEY_BLOCK), k_lanes]
            values = kv_ref[pl.ds(start, KEY_BLOCK), v_lanes]
            key_grad = value_grad = 0.0
            for j in range(per):
                h = part * per + j
                own = slice(h * head_dim, (h + 1) * head_dim)
                queries = own_lanes(q_ref[:, k_lanes], j, head_dim)
                grads = own_lanes(dout_ref[:, k_lanes], j, head_dim)
                scores = dot_nt(keys, queries)
                probs = jnp.where(allowed, jnp.exp(scores - lse_ref[h : h + 1, :]), 0.0)
                prob_grad = dot_nt(values, grads)
                value_grad = value_grad + dot(probs.astype(BF), grads)
                score_grad = (probs * (prob_grad - delta_ref[h : h + 1, :])).astype(BF)
                key_grad = key_grad + dot(score_grad, queries)
                product = dot_tn(keys, score_grad)[j * head_dim : (j + 1) * head_dim, :]
                acc_ref[own, :] = acc_ref[own, :] + product
            dkv_ref[pl.ds(start, KEY_BLOCK), k_lanes] = key_grad.astype(BF)
            dkv_ref[pl.ds(start, KEY_BLOCK), v_lanes] = value_grad.astype(BF)

    key_blocks(ranges, own_rows, rows, visit)
    for part in range(width // lanes):
        own = slice(part * lanes, (part + 1) * lanes)
        dq_ref[:, own] = acc_ref[own, :].T * (1.0 / math.sqrt(head_dim))


SMEM = pl.BlockSpec(memory_space=pltpu.SMEM)
WHOLE = pl.BlockSpec(memory_space=pltpu.VMEM)


def join_kernel(rows, seq_ref, even_ref, odd_ref, out_ref):
    for core, source in enumerate((even_ref, odd_ref)):
        for i in range(source.shape[0] // rows):
            start = pl.multiple_of((seq_ref[0] ^ (2 * i + core)) * rows, rows)
            out_ref[pl.ds(start, rows), :] = source[i * rows : (i + 1) * rows, :]


def join_columns_kernel(rows, seq_ref, even_ref, odd_ref, out_ref):
    lanes = even_ref.shape[1]
    for core, source in enumerate((even_ref, odd_ref)):
        for i in range(source.shape[0] // rows):
            start = pl.multiple_of((seq_ref[0] ^ (2 * i + core)) * lanes, lanes)
            piece = source[i * rows : (i + 1) * rows, :]
            out_ref[:, pl.ds(start, lanes)] = piece.astype(out_ref.dtype)


def place(even, odd, seq, dim, dtype):
    chips = lax.axis_size("seq") // 2
    rows = even.shape[0] // chips
    kernel = join_kernel if dim == 0 else join_columns_kernel
    shape = (2 * even.shape[0], even.shape[1])
    if dim == 1:
        shape = (rows, 2 * chips * even.shape[1])
    return pl.pallas_call(
        functools.partial(kernel, rows),
        out_shape=jax.ShapeDtypeStruct(shape, dtype),
        in_specs=[SMEM] + [WHOLE] * 2,
        out_specs=WHOLE,
        compiler_params=pltpu.CompilerParams(vmem_limit_bytes=VMEM_BYTES),
    )(jnp.reshape(seq, (1,)).astype(jnp.int32), even, odd)


def kernel_call(kernel, outputs, scratch, smem, arrays, work):
    return pl.pallas_call(
        kernel,
        out_shape=tuple(jax.ShapeDtypeStruct(shape, dtype) for shape, dtype in outputs),
        in_specs=[SMEM] * len(smem) + [WHOLE] * len(arrays),
        out_specs=(WHOLE,) * len(outputs),
        scratch_shapes=[pltpu.VMEM(shape, dtype) for shape, dtype in scratch],
        compiler_params=pltpu.CompilerParams(vmem_limit_bytes=VMEM_BYTES),
        cost_estimate=pl.CostEstimate(
            flops=work, bytes_accessed=sum(a.size * 2 for a in arrays), transcendentals=0
        ),
    )(*smem, *arrays)


def self_forward(ranges, queries, kv, meta, head_dim, lanes, own_rows):
    rows, width = queries.shape
    return kernel_call(
        functools.partial(self_forward_kernel, head_dim, lanes, own_rows),
        [((rows, width), F32), ((8, rows), F32)],
        [((8, rows), F32), ((8, rows), F32), ((width, rows), F32)],
        [ranges],
        [queries, kv, meta],
        KERNEL_WORK * rows * kv.shape[0] * width,
    )


def cross_forward(ranges, gates, queries, tkv, meta, self_out, head_dim, lanes):
    rows, width = queries.shape
    return kernel_call(
        functools.partial(cross_forward_kernel, head_dim, lanes),
        [((rows, width), BF), ((rows, width), F32), ((8, rows), F32)],
        [((width, rows), F32)],
        [ranges, gates],
        [queries, tkv, meta, self_out],
        KERNEL_WORK * rows * CAP * width,
    )


def cross_backward(ranges, gates, queries, tkv, meta, dout, lse, head_dim, lanes):
    rows, width = queries.shape
    return kernel_call(
        functools.partial(cross_backward_kernel, head_dim, lanes),
        [((width, rows), F32), (tkv.shape, BF)],
        [((rows, width), BF)],
        [ranges, gates],
        [queries, tkv, meta, dout, lse],
        2 * KERNEL_WORK * rows * CAP * width,
    )


def self_backward(ranges, queries, kv, meta, dout, self_out, lse, start, head_dim, lanes, own_rows):
    rows, width = queries.shape
    return kernel_call(
        functools.partial(self_backward_kernel, head_dim, lanes, own_rows),
        [((rows, width), F32), (kv.shape, BF)],
        [((8, rows), F32), ((width, rows), F32)],
        [ranges],
        [queries, kv, meta, dout, self_out, lse, start],
        2 * KERNEL_WORK * rows * kv.shape[0] * width,
    )


def body(
    video,
    conditioning,
    captions,
    clip_lengths,
    cap_lengths,
    positions,
    ada_weight,
    ada_bias,
    query_weight,
    key_weight,
    value_weight,
    out_weight,
    text_key_weight,
    text_value_weight,
    gate_weight,
    up_weight,
    down_weight,
    attn_gain,
    query_gain,
    key_gain,
    text_key_gain,
    attn_out_gain,
    ffn_gain,
    ffn_out_gain,
    cross_gate,
    cotangent,
):
    num_sub = lax.axis_size("sub")
    num_seq = lax.axis_size("seq")
    rows, width = video.shape
    heads_total = cross_gate.shape[0]
    head_dim = width // heads_total
    heads = heads_total // num_sub
    cols = width // num_sub
    device = lax.axis_index(BOTH)
    seq = lax.axis_index("seq")
    sub = lax.axis_index("sub")
    group = rows * num_sub
    tokens = group * num_seq
    clips = clip_lengths.shape[0]
    clip_range = jnp.arange(clips, dtype=jnp.int32)
    score_scale = 1.0 / math.sqrt(head_dim)

    ends = jnp.cumsum(clip_lengths)
    starts = ends - clip_lengths
    member = jnp.arange(group, dtype=jnp.int32)
    group_token = (seq * num_sub + (sub ^ (member // rows))) * rows + member % rows
    group_clip = clip_index(group_token, clip_lengths)
    group_hot_bool = group_clip[:, None] == clip_range[None, :]
    group_hot = group_hot_bool.astype(F32)
    own_hot = group_hot[:rows]
    first = jnp.sum(jnp.where(group_hot_bool, starts[None, :], 0), 1)
    last = jnp.sum(jnp.where(group_hot_bool, ends[None, :], 0), 1)
    meta = jnp.concatenate(
        [first[None], last[None], group_clip[None], jnp.zeros((5, group), jnp.int32)], 0
    )
    ranges = jnp.concatenate(
        [
            jnp.stack(
                [
                    jnp.min(first) // KEY_BLOCK,
                    (jnp.max(last) + KEY_BLOCK - 1) // KEY_BLOCK,
                    jnp.min(group_clip),
                    jnp.max(group_clip) + 1,
                    seq,
                    sub,
                ]
            ).astype(jnp.int32),
            cap_lengths,
        ]
    )
    gate_tanh = jnp.tanh(cross_gate.astype(F32))
    gates = lax.dynamic_slice_in_dim(gate_tanh, sub * heads, heads, 0)

    cond_float = conditioning.astype(F32)
    cond_act = jax.nn.silu(cond_float).astype(BF)
    cond_rows = ada_weight.shape[0]
    cond_slice = lax.dynamic_slice_in_dim(cond_act, device * cond_rows, cond_rows, 1)
    mod_part = dot(cond_slice, ada_weight)
    mod_part = mod_part + lax.dynamic_update_slice_in_dim(
        jnp.zeros((1, 4 * width), F32), ada_bias.astype(F32)[None], device * ada_bias.shape[0], 1
    )
    mod_part = mod_part.reshape(clips, 4, width)
    gain_rows = attn_gain.shape[0]

    def spread(gains):
        stacked = jnp.stack(gains).astype(F32)
        return lax.dynamic_update_slice_in_dim(
            jnp.zeros((len(gains), width), F32), stacked, device * gain_rows, 1
        )

    order = Schedule()
    out_full = gather_rows(out_weight, BOTH)
    early_flow = Flow(
        total_cube(
            jnp.concatenate([mod_part[:, 0], spread([attn_gain, query_gain, key_gain])], 0),
            ("seq", "sub"),
        )
    )
    late_flow = Flow(
        total_cube(
            jnp.concatenate(
                [
                    mod_part[:, 1],
                    mod_part[:, 2],
                    mod_part[:, 3],
                    spread([text_key_gain, attn_out_gain, ffn_gain, ffn_out_gain]),
                ],
                0,
            ),
            ("seq", "sub"),
        )
    )
    w_rows = query_weight.shape[0]
    qkv_blocks = [
        jnp.concatenate(parts, 1)
        for parts in zip(*[blocks_for(w, 1) for w in (query_weight, key_weight, value_weight)])
    ]
    flow = Flow(swap_direct(qkv_blocks))
    order.step(flow, early_flow)
    packed = jnp.concatenate(
        [video, jnp.pad(positions.astype(BF), ((0, 0), (0, 128 - positions.shape[1])))], 1
    )
    packed = swap_copies(order.tie(packed)[0]).reshape(num_sub * rows, -1)
    flow = Flow(gather_seq(jnp.concatenate(in_order(flow.result, sub), 0)))
    while not (flow.done and early_flow.done):
        order.step(flow, early_flow)
    qkv_weight = flow.result
    early = early_flow.result
    scale_rows = early[:clips]
    attn_gain_f = early[clips : clips + 1]
    query_gain_f = lax.dynamic_slice_in_dim(early[clips + 1 : clips + 2], sub * cols, cols, 1)
    key_gain_f = lax.dynamic_slice_in_dim(early[clips + 2 : clips + 3], sub * cols, cols, 1)
    packed = jnp.concatenate(blocks_for(packed, 0), 0)
    video_group = packed[:, :width].astype(F32)
    group_pos = packed[:, width : width + 3].astype(F32)
    cap_shard = captions.shape[0]
    cap_total = cap_shard * num_sub
    t_rows = text_key_weight.shape[0]
    t_block = num_sub * t_rows
    cap_block = lax.dynamic_slice_in_dim(captions, seq * t_block, t_block, 1)
    cap_block = lax.optimization_barrier((cap_block, packed))[0]
    cap_block = swap_copies(cap_block).reshape(cap_total, t_block)
    text_weight = jnp.stack(
        [
            jnp.concatenate(
                [w[:, i * cols : (i + 1) * cols] for w in (text_key_weight, text_value_weight)], 1
            )
            for i in range(num_sub)
        ]
    )
    text_weight = lax.optimization_barrier((text_weight, cap_block))[0]
    text_weight = swap_blocks(text_weight, "sub").reshape(t_block, 2 * cols)

    video_inv = inv_rms(video_group)
    video_hat = video_group * video_inv
    attn_scale1 = 1.0 + pick_rows(group_hot, scale_rows)
    normed = (video_hat * (attn_gain_f * attn_scale1)).astype(BF)
    qkv_pre = dot(normed, qkv_weight)
    query_pre = qkv_pre[:, :cols]
    key_pre = qkv_pre[:, cols : 2 * cols]
    flow = Flow(
        total_rows(
            jnp.stack([jnp.sum(query_pre * query_pre, 1), jnp.sum(key_pre * key_pre, 1)])
        )
    )
    order.step(flow)
    inverse = lax.rsqrt(flow.result / width + epsilon)
    query_inv = inverse[0].reshape(group, 1)
    key_inv = inverse[1].reshape(group, 1)
    query_hat = query_pre * query_inv
    key_hat = key_pre * key_inv
    cosine, sine = rope_tables(group_pos, head_dim, heads)
    queries = (rotate(query_hat * query_gain_f, cosine, sine).astype(BF) * score_scale).astype(BF)
    keys = rotate(key_hat * key_gain_f, cosine, sine).astype(BF)
    values = qkv_pre[:, 2 * cols :].astype(BF)
    lanes = 2 * head_dim if heads % 2 == 0 else head_dim
    parts = [slice(i * lanes, (i + 1) * lanes) for i in range(cols // lanes)]
    kv = gather_rows(order.tie(jnp.concatenate([keys, values], 1))[0], "seq")

    units = gate_weight.shape[1] // num_seq
    gate_up = jnp.stack(
        [
            jnp.concatenate(
                [w[:, i * units : (i + 1) * units] for w in (gate_weight, up_weight)], 1
            )
            for i in range(num_seq)
        ]
    )
    (gate_up,) = order.tie(gate_up)
    gate_up = swap_blocks(gate_up, "seq").reshape(num_seq * w_rows, 2 * units)
    gate_up = gather_rows(lax.optimization_barrier((gate_up, kv))[0], "sub")
    gate_up = (
        gate_up.reshape(num_sub, num_seq, w_rows, 2 * units)
        .transpose(1, 0, 2, 3)
        .reshape(width, 2 * units)
    )
    down_block = lax.optimization_barrier((down_weight, text_weight))[0]
    down_block = gather_rows(down_block, "sub")

    slots = cap_total // num_seq
    text_parts = {}

    def text_chain():
        part = dot(cap_block, text_weight).astype(BF)
        pre = yield from scatter_seq(part)
        key_pre = pre[:, :cols]
        square = yield from total(jnp.sum(key_pre * key_pre, 1)[None], ("sub",))
        inv = lax.rsqrt(square / width + epsilon).reshape(slots, 1)
        text_parts["inv"], text_parts["hat"] = inv, key_pre * inv
        gain = lax.dynamic_slice_in_dim(
            late_flow.result[3 * clips : 3 * clips + 1], sub * cols, cols, 1
        )
        text_parts["gain"] = gain
        gathered = yield from gather_seq(
            jnp.concatenate([(key_pre * inv * gain).astype(BF), pre[:, cols:].astype(BF)], 1)
        )
        return gathered

    for _ in range(len(axis_bits("seq")) + len(axis_bits("sub")) - 3):
        order.step(late_flow)
    text_flow = Flow(text_chain())
    for _ in range(3):
        order.step(late_flow, text_flow)
    self_out, lse = order.step(
        text_flow,
        work=lambda *a: self_forward(ranges, *a, meta, head_dim, lanes, rows),
        args=(queries, kv),
    )
    while not (text_flow.done and late_flow.done):
        order.step(text_flow, late_flow)
    tkv = text_flow.result
    text_inv, text_hat, text_key_gain_f = (text_parts[k] for k in ("inv", "hat", "gain"))
    late = late_flow.result
    attn_gate = pick_rows(own_hot, late[:clips])
    ffn_scale = pick_rows(own_hot, late[clips : 2 * clips])
    ffn_gate = pick_rows(own_hot, late[2 * clips : 3 * clips])
    attn_out_f = late[3 * clips + 1 : 3 * clips + 2]
    ffn_gain_f = late[3 * clips + 2 : 3 * clips + 3]
    ffn_out_f = late[3 * clips + 3 : 3 * clips + 4]

    mixed_heads, cross_out, cross_lse = cross_forward(
        ranges, gates, queries, tkv, meta, self_out, head_dim, lanes
    )
    flow = Flow(swap_direct([mixed_heads[i * rows : (i + 1) * rows] for i in range(num_sub)]))
    order.step(flow)
    mixed = jnp.concatenate(in_order(flow.result, sub), 1)

    def run(flow):
        while not flow.done:
            order.step(flow)
        return flow.result

    video_own = video.astype(F32)
    projected = dot(mixed, out_full)
    proj_inv = inv_rms(projected)
    proj_hat = projected * proj_inv
    attn_tanh = jnp.tanh(attn_gate)
    hidden_state = video_own + attn_tanh * proj_hat * attn_out_f
    hidden_inv = inv_rms(hidden_state)
    hidden_hat = hidden_state * hidden_inv
    ffn_mult = ffn_gain_f * (1.0 + ffn_scale)
    ffn_in = jnp.concatenate(run(Flow(gather_even_odd((hidden_hat * ffn_mult).astype(BF)))), 0)
    half = ffn_in.shape[0] // 2
    gate_up_pre = dot(ffn_in, gate_up)
    gate_pre = gate_up_pre[:, :units]
    up_pre = gate_up_pre[:, units:]
    gate_sig = jax.nn.sigmoid(gate_pre)
    gate_act = gate_pre * gate_sig
    activated = (gate_act * up_pre).astype(BF)
    down_part = dot(activated, down_block).astype(BF)
    down_out = run(Flow(scatter_even_odd(down_part[:half], down_part[half:])))
    down_inv = inv_rms(down_out)
    down_hat = down_out * down_inv
    ffn_tanh = jnp.tanh(ffn_gate)
    block_out = (hidden_state + ffn_tanh * down_hat * ffn_out_f).astype(BF)

    grad_out = cotangent.astype(F32)
    ffn_gate_grad = grad_out * down_hat * ffn_out_f * (1.0 - ffn_tanh * ffn_tanh)
    ffn_out_gain_part = jnp.sum(grad_out * ffn_tanh * down_hat, 0)
    down_grad = norm_back(down_hat, down_inv, grad_out * ffn_tanh * ffn_out_f).astype(BF)
    down_grad = jnp.concatenate(run(Flow(gather_even_odd(down_grad))), 0)
    act_grad = dot_nt(down_grad, down_block)
    gate_grad = (act_grad * up_pre * gate_sig * (1.0 + gate_pre * (1.0 - gate_sig))).astype(BF)
    up_grad = (act_grad * gate_act).astype(BF)
    gate_up_grad = jnp.concatenate([gate_grad, up_grad], 1)
    ffn_in_part = dot_nt(gate_up_grad, gate_up).astype(BF)
    ffn_in_grad = run(Flow(scatter_even_odd(ffn_in_part[:half], ffn_in_part[half:])))
    down_weight_term = dot_tn(activated, down_grad).astype(BF)
    down_weight_grad = scatter_rows(down_weight_term, "sub").astype(F32)
    gate_up_term = dot_tn(ffn_in, gate_up_grad).astype(BF)
    gate_up_term = (
        gate_up_term.reshape(num_seq, num_sub, w_rows, 2 * units)
        .transpose(1, 0, 2, 3)
        .reshape(width, 2 * units)
    )
    gate_up_term = scatter_rows(gate_up_term, "sub").reshape(num_seq, w_rows, 2 * units)

    ffn_gain_part = jnp.sum(ffn_in_grad * hidden_hat * (1.0 + ffn_scale), 0)
    ffn_scale_grad = ffn_in_grad * hidden_hat * ffn_gain_f
    hidden_grad = grad_out + norm_back(hidden_hat, hidden_inv, ffn_in_grad * ffn_mult)
    attn_gate_grad = hidden_grad * proj_hat * attn_out_f * (1.0 - attn_tanh * attn_tanh)
    attn_out_gain_part = jnp.sum(hidden_grad * attn_tanh * proj_hat, 0)
    proj_grad = norm_back(proj_hat, proj_inv, hidden_grad * attn_tanh * attn_out_f).astype(BF)
    mixed_grad = dot_nt(proj_grad, out_full).astype(BF)
    out_weight_term = dot_tn(mixed, proj_grad).astype(BF)
    flow = Flow(swap_direct(blocks_for(mixed_grad, 1)))
    order.step(flow)
    dout = jnp.concatenate(flow.result, 0)
    cross_gate_part = jnp.sum(
        (dout.astype(F32) * cross_out).reshape(group, heads, head_dim), (0, 2)
    ) * (1.0 - gates * gates)

    def clip_sums(values):
        return dot_tn(own_hot.astype(BF), values.astype(BF))

    def at_columns(part):
        return lax.dynamic_update_slice_in_dim(
            jnp.zeros((1, width), F32), part.reshape(1, -1), sub * cols, 1
        )

    gate_row = lax.dynamic_update_slice_in_dim(
        jnp.zeros((1, width), F32), cross_gate_part.reshape(1, -1), sub * heads, 1
    )
    late_flow = Flow(
        total_cube(
            jnp.concatenate(
                [
                    clip_sums(attn_gate_grad),
                    clip_sums(ffn_scale_grad),
                    clip_sums(ffn_gate_grad),
                    attn_out_gain_part[None],
                    ffn_gain_part[None],
                    ffn_out_gain_part[None],
                    gate_row,
                ],
                0,
            ),
            ("seq", "sub"),
        )
    )
    query_start, dtkv = cross_backward(
        ranges, gates, queries, tkv, meta, dout, cross_lse, head_dim, lanes
    )
    text_flow = Flow(scatter_seq(dtkv))
    def text_back_chain():
        reduced = yield from scatter_seq(dtkv)
        low = reduced[:, :cols].astype(BF).astype(F32)
        hat_grad = low * text_key_gain_f
        inner = yield from total(jnp.sum(text_hat * hat_grad, 1)[None], ("sub",))
        text_parts["gain"] = jnp.sum(low * text_hat, 0)
        pre_grad = text_inv * (hat_grad - text_hat * (inner / width).reshape(slots, 1))
        gathered = yield from gather_seq(
            jnp.concatenate([pre_grad.astype(BF), reduced[:, cols:].astype(BF)], 1)
        )
        return gathered

    text_flow = Flow(text_back_chain())
    query_rot_grad, dkv = order.step(
        text_flow,
        late_flow,
        work=lambda *a: self_backward(ranges, a[0], a[1], meta, *a[2:], head_dim, lanes, rows),
        args=(queries, kv, dout, self_out, lse, query_start),
    )
    dkv = scatter_rows(dkv, "seq")
    out_weight_term = lax.optimization_barrier((out_weight_term, dkv))[0]
    out_weight_grad = scatter_rows(scatter_rows(out_weight_term, "seq"), "sub").astype(F32)
    while not (text_flow.done and late_flow.done):
        order.step(text_flow, late_flow)
    text_key_gain_part = text_parts["gain"]
    text_grad = text_flow.result
    query_rot_grad = query_rot_grad.astype(BF).astype(F32)
    key_rot_grad = dkv[:, :cols].astype(F32)
    value_grad = dkv[:, cols:]
    query_norm_grad = rotate(query_rot_grad, cosine, -sine)
    query_gain_part = jnp.sum(query_norm_grad * query_hat, 0)
    query_hat_grad = query_norm_grad * query_gain_f
    key_norm_grad = rotate(key_rot_grad, cosine, -sine)
    key_gain_part = jnp.sum(key_norm_grad * key_hat, 0)
    key_hat_grad = key_norm_grad * key_gain_f
    flow = Flow(
        total_rows(
            jnp.stack(
                [jnp.sum(query_hat * query_hat_grad, 1), jnp.sum(key_hat * key_hat_grad, 1)]
            )
        )
    )
    order.step(flow)
    inner = flow.result / width
    caption_part = dot_nt(text_grad, text_weight).astype(BF).reshape(num_sub, cap_shard, t_block)
    text_term = dot_tn(cap_block, text_grad).astype(BF).reshape(num_sub, t_rows, 2 * cols)
    query_pre_grad = query_inv * (query_hat_grad - query_hat * inner[0].reshape(group, 1))
    key_pre_grad = key_inv * (key_hat_grad - key_hat * inner[1].reshape(group, 1))
    qkv_grad = jnp.concatenate([query_pre_grad.astype(BF), key_pre_grad.astype(BF), value_grad], 1)
    qkv_term = dot_tn(normed, qkv_grad).astype(BF)
    normed_part = dot_nt(qkv_grad, qkv_weight)

    hat_grad = normed_part * video_hat
    attn_gain_part = jnp.sum(hat_grad * attn_scale1, 0)
    scale_part = dot_tn(group_hot.astype(BF), (hat_grad * attn_gain_f).astype(BF))
    early_flow = Flow(
        total(
            jnp.concatenate(
                [
                    scale_part,
                    attn_gain_part[None],
                    at_columns(query_gain_part),
                    at_columns(key_gain_part),
                    at_columns(text_key_gain_part),
                ],
                0,
            ),
            ("seq", "sub"),
        )
    )
    qkv_flow = Flow(scatter_seq(qkv_term))
    caption_block = jnp.sum(
        swap_blocks(order.tie(caption_part)[0], "sub").astype(F32), 0
    ).astype(BF)
    normed_low = jnp.concatenate(blocks_for(normed_part.astype(BF), 0), 0)
    normed_grad = scatter_rows(order.tie(normed_low)[0], "sub").astype(F32)
    text_term = lax.optimization_barrier((text_term, normed_grad))[0]
    text_term = swap_blocks(text_term, "sub")
    caption_flow = Flow(gather_seq(caption_block, 1, F32))
    order.step(early_flow, qkv_flow)
    order.step(early_flow, qkv_flow)
    order.step(early_flow)
    late_sum = late_flow.result
    early_sum = early_flow.result
    mod_low = jnp.concatenate(
        [
            early_sum[:clips],
            late_sum[:clips],
            late_sum[clips : 2 * clips],
            late_sum[2 * clips : 3 * clips],
        ],
        1,
    ).astype(BF)
    cond_part = lax.dynamic_update_slice_in_dim(
        jnp.zeros(conditioning.shape, F32), dot_nt(mod_low, ada_weight), device * cond_rows, 1
    )
    cond_flow = Flow(total(cond_part, ("seq", "sub")))
    qkv_term = order.tie(qkv_flow.result.astype(BF).reshape(num_sub, w_rows, 3 * cols))[0]
    qkv_term = swap_blocks(qkv_term, "sub")
    order.step(caption_flow)
    order.step(cond_flow, caption_flow)
    order.step(cond_flow)
    order.step(cond_flow)
    caption_grad = caption_flow.result
    query_weight_grad, key_weight_grad, value_weight_grad = (
        jnp.concatenate([block[:, j * cols : (j + 1) * cols] for block in qkv_term], 1).astype(F32)
        for j in range(3)
    )
    text_key_weight_grad, text_value_weight_grad = (
        jnp.concatenate([block[:, j * cols : (j + 1) * cols] for block in text_term], 1).astype(F32)
        for j in range(2)
    )
    gate_up_term = swap_blocks(gate_up_term, "seq")
    gate_weight_grad, up_weight_grad = (
        jnp.concatenate(
            [gate_up_term[i, :, j * units : (j + 1) * units] for i in range(num_seq)], 1
        ).astype(F32)
        for j in range(2)
    )

    own_hat, own_inv, own_scale1 = video_hat[:rows], video_inv[:rows], attn_scale1[:rows]
    video_grad = hidden_grad + norm_back(own_hat, own_inv, normed_grad * (attn_gain_f * own_scale1))

    def own_gain(row):
        return lax.dynamic_slice_in_dim(row, device * gain_rows, gain_rows, 0)

    bias_rows = ada_bias.shape[0]
    ada_bias_grad = jnp.sum(
        lax.dynamic_slice_in_dim(mod_low.astype(F32), device * bias_rows, bias_rows, 1), 0
    )
    ada_weight_grad = dot_tn(cond_slice, mod_low)
    cond_sig = jax.nn.sigmoid(cond_float)
    cond_grad = cond_flow.result * cond_sig * (1.0 + cond_float * (1.0 - cond_sig))
    return (
        block_out,
        video_grad,
        caption_grad,
        cond_grad,
        ada_weight_grad,
        ada_bias_grad,
        query_weight_grad,
        key_weight_grad,
        value_weight_grad,
        out_weight_grad,
        text_key_weight_grad,
        text_value_weight_grad,
        gate_weight_grad,
        up_weight_grad,
        down_weight_grad,
        own_gain(early_sum[clips]),
        own_gain(early_sum[clips + 1]),
        own_gain(early_sum[clips + 2]),
        own_gain(early_sum[clips + 3]),
        own_gain(late_sum[3 * clips]),
        own_gain(late_sum[3 * clips + 1]),
        own_gain(late_sum[3 * clips + 2]),
        late_sum[3 * clips + 3, :heads_total],
    )


def solution(mesh):
    matrix = P(BOTH, None)
    vector = P(BOTH)
    return jax.shard_map(
        body,
        mesh=mesh,
        in_specs=(matrix, P(), P("sub", None), P(), P(), matrix, matrix, vector)
        + (matrix,) * 9
        + (vector,) * 7
        + (P(), matrix),
        out_specs=(matrix, matrix, P("sub", None), P(), matrix, vector)
        + (matrix,) * 9
        + (vector,) * 7
        + (P(),),
        check_vma=False,
    )
```

```python
import functools
import math

import jax
import jax.numpy as jnp
import numpy as np
from jax import lax
from jax.experimental import pallas as pl
from jax.experimental.pallas import tpu as pltpu
from jax.sharding import PartitionSpec as P

CAP = 256
KEY_BLOCK = 512
epsilon = 1e-06
rope_base = 10000.0
masked_score = -1e30
BF = jnp.bfloat16
F32 = jnp.float32
BOTH = ("seq", "sub")
VMEM_BYTES = 56 * 1024 * 1024
KERNEL_WORK = 16


def axis_bits(axis):
    masks, mask = [], 1
    while mask < lax.axis_size(axis):
        masks.append(mask)
        mask *= 2
    return masks


def send(values, axis, mask):
    count = lax.axis_size(axis)
    return lax.ppermute(values, axis, [(i, i ^ mask) for i in range(count)])


class Flow:
    def __init__(self, stages):
        self.stages = stages
        self.result = None
        self.done = False
        self.wanted = next(stages)

    def feed(self, arrived):
        try:
            self.wanted = self.stages.send(arrived)
        except StopIteration as stop:
            self.wanted, self.done, self.result = [], True, stop.value


class Schedule:
    def __init__(self):
        self.frontier = ()

    def tie(self, *arrays):
        tied = lax.optimization_barrier(tuple(arrays) + self.frontier)
        return tied[: len(arrays)]

    def step(self, *flows, work=None, args=()):
        flows = [flow for flow in flows if not flow.done]
        sends = [item for flow in flows for item in flow.wanted]
        tied = self.tie(*[item[0] for item in sends], *args)
        arrived = [send(value, item[1], item[2]) for value, item in zip(tied, sends)]
        outputs = work(*tied[len(sends) :]) if work is not None else ()
        self.frontier = tuple(arrived) + tuple(jax.tree.leaves(outputs))
        for flow in flows:
            count = len(flow.wanted)
            flow.feed(arrived[:count])
            arrived = arrived[count:]
        return outputs

    def start(self, flow, *others):
        tied = lax.optimization_barrier(
            tuple(item[0] for item in flow.wanted) + self.frontier + tuple(others)
        )
        flow.feed([send(v, item[1], item[2]) for v, item in zip(tied, flow.wanted)])
        return flow.result

    def held(self, values):
        return list(self.tie(*values))


def in_order(pieces, index):
    mask = 1
    while mask < len(pieces):
        flip = (index // mask) % 2 == 1
        pieces = [jnp.where(flip, pieces[i ^ mask], pieces[i]) for i in range(len(pieces))]
        mask *= 2
    return pieces


def rows_in_order(pieces, index):
    shape = pieces[0][1].shape
    result = jnp.zeros((len(pieces),) + shape, pieces[0][1].dtype)
    for mask, piece in pieces:
        result = lax.dynamic_update_index_in_dim(result, piece, index ^ mask, 0)
    return result.reshape((len(pieces) * shape[0],) + shape[1:])


def gather_even_odd(values, axis="seq"):
    arrived = yield [(values, axis, mask) for mask in range(2, lax.axis_size(axis), 2)]
    even = jnp.concatenate([values] + arrived, 0)
    (odd,) = yield [(even, axis, 1)]
    return even, odd


def scatter_even_odd(even, odd, axis="seq"):
    count = lax.axis_size(axis) // 2
    rows = even.shape[0] // count
    (other,) = yield [(odd, axis, 1)]
    held = (even.astype(F32) + other.astype(F32)).astype(even.dtype)
    arrived = yield [
        (held[i * rows : (i + 1) * rows], axis, 2 * i) for i in range(1, count)
    ]
    result = held[:rows].astype(F32)
    for piece in arrived:
        result = result + piece.astype(F32)
    return result


def gather_seq(values, dim=0, dtype=None):
    even, odd = yield from gather_even_odd(values)
    return place(even, odd, lax.axis_index("seq"), dim, dtype or values.dtype)


def scatter_seq(values):
    index = lax.axis_index("seq")
    count = lax.axis_size("seq")
    blocks = values.reshape((count, values.shape[0] // count) + values.shape[1:])
    halves = [
        jnp.concatenate(
            [
                lax.dynamic_index_in_dim(blocks, index ^ mask, 0, keepdims=False)
                for mask in range(core, count, 2)
            ],
            0,
        )
        for core in range(2)
    ]
    result = yield from scatter_even_odd(*halves)
    return result


def pair_sum(pieces):
    while len(pieces) > 1:
        pieces = [pieces[i] + pieces[i + 1] for i in range(0, len(pieces), 2)]
    return pieces[0]


def total(values, axes):
    for axis in axes:
        groups = [range(1, lax.axis_size(axis))]
        if axis == "seq":
            groups = [range(2, lax.axis_size(axis), 2), [1]]
        for masks in groups:
            arrived = yield [(values, axis, mask) for mask in masks]
            values = pair_sum([values] + arrived)
    return values


def total_cube(values, axes):
    for axis in axes:
        for mask in axis_bits(axis):
            (other,) = yield [(values, axis, mask)]
            values = values + other
    return values


def total_rows(values, axis="sub"):
    count = lax.axis_size(axis)
    rows = values.shape[1] // count
    arrived = yield [(values, axis, mask) for mask in range(1, count)]
    for mask, other in enumerate(arrived, 1):
        values = values + jnp.concatenate(
            [other[:, (i ^ mask) * rows : ((i ^ mask) + 1) * rows] for i in range(count)], 1
        )
    return values


def gather_direct(values, axis="sub"):
    arrived = yield [(values, axis, mask) for mask in range(1, lax.axis_size(axis))]
    return [values] + arrived


def swap_direct(blocks, axis="sub"):
    arrived = yield [(blocks[mask], axis, mask) for mask in range(1, len(blocks))]
    return [blocks[0]] + arrived


def scatter_direct(blocks, axis="sub"):
    arrived = yield [(blocks[mask], axis, mask) for mask in range(1, len(blocks))]
    result = blocks[0].astype(F32)
    for other in arrived:
        result = result + other.astype(F32)
    return result


def blocks_for(values, dim, axis="sub"):
    index = lax.axis_index(axis)
    count = lax.axis_size(axis)
    size = values.shape[dim] // count
    if dim == 0:
        blocks = values.reshape((count, size) + values.shape[1:])
        return [
            lax.dynamic_index_in_dim(blocks, index ^ mask, 0, keepdims=False)
            for mask in range(count)
        ]
    return in_order([values[:, i * size : (i + 1) * size] for i in range(count)], index)


def swap_blocks(values, axis):
    return lax.all_to_all(values, axis, split_axis=0, concat_axis=0, tiled=True)


def swap_copies(values, axis="sub"):
    return swap_blocks(jnp.broadcast_to(values[None], (lax.axis_size(axis),) + values.shape), axis)


def gather_rows(values, axis):
    return lax.all_gather(values, axis, axis=0, tiled=True)


def scatter_rows(values, axis):
    return lax.psum_scatter(values, axis, scatter_dimension=0, tiled=True)


def inv_rms(values):
    return lax.rsqrt(jnp.mean(values * values, -1, keepdims=True) + epsilon)


def norm_back(normed_hat, inverse, grad_hat):
    return inverse * (grad_hat - normed_hat * jnp.mean(normed_hat * grad_hat, -1, keepdims=True))


def dot(left, right):
    return jnp.dot(left, right, preferred_element_type=F32)


def dot_nt(left, right):
    return lax.dot_general(left, right, (((1,), (1,)), ((), ())), preferred_element_type=F32)


def dot_tn(left, right):
    return lax.dot_general(left, right, (((0,), (0,)), ((), ())), preferred_element_type=F32)


def rope_tables(positions, head_dim, heads):
    pair_total = head_dim // 2
    frame_pairs = pair_total // 4
    height_pairs = (pair_total - frame_pairs) // 2
    width_pairs = pair_total - frame_pairs - height_pairs
    frequency = np.zeros((3, pair_total), np.float32)
    start = 0
    for axis_id, pair_count in enumerate((frame_pairs, height_pairs, width_pairs)):
        exponent = -np.arange(pair_count, dtype=np.float32) / np.float32(pair_count)
        frequency[axis_id, start : start + pair_count] = np.float32(rope_base) ** exponent
        start += pair_count
    frequency = jnp.asarray(np.repeat(frequency, 2, axis=1))
    angles = (
        positions[:, 0:1] * frequency[0:1]
        + positions[:, 1:2] * frequency[1:2]
        + positions[:, 2:3] * frequency[2:3]
    )
    sign = jnp.asarray(np.where(np.arange(head_dim) % 2 == 0, -1.0, 1.0).astype(np.float32))
    cosine = jnp.cos(angles)
    sine = jnp.sin(angles) * sign[None, :]
    return (jnp.tile(cosine, (1, heads)), jnp.tile(sine, (1, heads)))


def rotate(values, cosine, sine):
    even = lax.broadcasted_iota(jnp.int32, values.shape, 1) % 2 == 0
    swapped = jnp.where(even, jnp.roll(values, -1, 1), jnp.roll(values, 1, 1))
    return values * cosine + swapped * sine


def clip_index(token_index, clip_lengths):
    bounds = jnp.cumsum(clip_lengths)
    return jnp.sum((token_index[:, None] >= bounds[None, :]).astype(jnp.int32), 1)


def pick_rows(onehot, rows):
    picked = onehot[:, 0:1] * rows[0:1]
    for clip in range(1, rows.shape[0]):
        picked = picked + onehot[:, clip : clip + 1] * rows[clip : clip + 1]
    return picked


def own_lanes(block, head, head_dim):
    if block.shape[1] == head_dim:
        return block
    lane = lax.broadcasted_iota(jnp.int32, block.shape, 1)
    return jnp.where(lane // head_dim == head, block, jnp.zeros_like(block))


def key_blocks(ranges, own_rows, rows, visit):
    per_group = rows // KEY_BLOCK
    per_block = KEY_BLOCK // own_rows

    def step(place, carry):
        block = (place // per_group) * per_group
        block = block + ((place % per_group) ^ (ranges[5] // per_block))
        row = lax.broadcasted_iota(jnp.int32, (KEY_BLOCK, rows), 0)
        index = place * KEY_BLOCK + (row ^ ((ranges[5] % per_block) * own_rows))
        visit(pl.multiple_of(block * KEY_BLOCK, KEY_BLOCK), index)
        return carry

    lax.fori_loop(ranges[0], ranges[1], step, 0)


def self_forward_kernel(
    head_dim,
    lanes,
    own_rows,
    ranges,
    q_ref,
    kv_ref,
    meta_ref,
    self_ref,
    lse_ref,
    max_ref,
    sum_ref,
    acc_ref,
):
    rows, width = q_ref.shape
    per = lanes // head_dim
    max_ref[...] = jnp.full(max_ref.shape, masked_score, F32)
    sum_ref[...] = jnp.zeros(sum_ref.shape, F32)
    acc_ref[...] = jnp.zeros(acc_ref.shape, F32)
    first = meta_ref[0:1, :]
    last = meta_ref[1:2, :]

    def visit(start, key_index):
        allowed = (key_index >= first) & (key_index < last)
        for part in range(width // lanes):
            k_lanes = slice(part * lanes, (part + 1) * lanes)
            keys = kv_ref[pl.ds(start, KEY_BLOCK), k_lanes]
            values = kv_ref[pl.ds(start, KEY_BLOCK), width + part * lanes : width + (part + 1) * lanes]
            for j in range(per):
                h = part * per + j
                own = slice(h * head_dim, (h + 1) * head_dim)
                queries = own_lanes(q_ref[:, k_lanes], j, head_dim)
                scores = jnp.where(allowed, dot_nt(keys, queries), masked_score)
                old_max = max_ref[h : h + 1, :]
                new_max = jnp.maximum(old_max, jnp.max(scores, 0, keepdims=True))
                probs = jnp.exp(scores - new_max)
                factor = jnp.exp(old_max - new_max)
                max_ref[h : h + 1, :] = new_max
                sum_ref[h : h + 1, :] = sum_ref[h : h + 1, :] * factor + jnp.sum(
                    probs, 0, keepdims=True
                )
                product = dot_tn(values, probs.astype(BF))[j * head_dim : (j + 1) * head_dim, :]
                acc_ref[own, :] = acc_ref[own, :] * factor + product

    key_blocks(ranges, own_rows, rows, visit)
    lse_ref[...] = jnp.zeros(lse_ref.shape, F32)
    for h in range(width // head_dim):
        own = slice(h * head_dim, (h + 1) * head_dim)
        sums = sum_ref[h : h + 1, :]
        acc_ref[own, :] = acc_ref[own, :] / sums
        lse_ref[h : h + 1, :] = max_ref[h : h + 1, :] + jnp.log(sums)
    for part in range(width // lanes):
        own = slice(part * lanes, (part + 1) * lanes)
        self_ref[:, own] = acc_ref[own, :].T


def cross_forward_kernel(
    head_dim, lanes, ranges, gates, q_ref, tkv_ref, meta_ref, self_ref, mixed_ref, cross_ref, lse_ref, acc_ref
):
    rows, width = q_ref.shape
    acc_ref[...] = jnp.zeros(acc_ref.shape, F32)
    lse_ref[...] = jnp.zeros(lse_ref.shape, F32)
    clip = meta_ref[2:3, :]
    per = lanes // head_dim

    def step(which, carry):
        start = pl.multiple_of(which * CAP, CAP)
        slot = lax.broadcasted_iota(jnp.int32, (CAP, rows), 0)
        valid = slot < ranges[6 + which]
        here = clip == which
        for part in range(width // lanes):
            keys = tkv_ref[pl.ds(start, CAP), part * lanes : (part + 1) * lanes]
            values = tkv_ref[pl.ds(start, CAP), width + part * lanes : width + (part + 1) * lanes]
            queries = q_ref[:, part * lanes : (part + 1) * lanes]
            for j in range(per):
                h = part * per + j
                own = slice(h * head_dim, (h + 1) * head_dim)
                scores = dot_nt(keys, own_lanes(queries, j, head_dim))
                scores = jnp.where(valid, scores, masked_score)
                top = jnp.max(scores, 0, keepdims=True)
                probs = jnp.exp(scores - top)
                sums = jnp.sum(probs, 0, keepdims=True)
                probs = (probs / sums).astype(BF)
                product = dot_tn(values, probs)[j * head_dim : (j + 1) * head_dim, :]
                acc_ref[own, :] = jnp.where(here, product, acc_ref[own, :])
                lse_ref[h : h + 1, :] = jnp.where(here, top + jnp.log(sums), lse_ref[h : h + 1, :])
        return carry

    lax.fori_loop(ranges[2], ranges[3], step, 0)
    lane = lax.broadcasted_iota(jnp.int32, (1, lanes), 1)
    for part in range(width // lanes):
        own = slice(part * lanes, (part + 1) * lanes)
        cross = acc_ref[own, :].T
        gate = jnp.full((1, lanes), gates[part * per], F32)
        for j in range(1, per):
            gate = jnp.where(lane // head_dim == j, gates[part * per + j], gate)
        cross_ref[:, own] = cross
        mixed_ref[:, own] = (self_ref[:, own].astype(BF).astype(F32) + gate * cross).astype(BF)


def cross_backward_kernel(
    head_dim, lanes, ranges, gates, q_ref, tkv_ref, meta_ref, dout_ref, lse_ref, acc_ref, dtkv_ref, gated_ref
):
    rows, width = q_ref.shape
    per = lanes // head_dim
    dtkv_ref[...] = jnp.zeros(dtkv_ref.shape, dtkv_ref.dtype)
    acc_ref[...] = jnp.zeros(acc_ref.shape, F32)
    lane = lax.broadcasted_iota(jnp.int32, (1, lanes), 1)
    for part in range(width // lanes):
        own = slice(part * lanes, (part + 1) * lanes)
        gate = jnp.full((1, lanes), gates[part * per], F32)
        for j in range(1, per):
            gate = jnp.where(lane // head_dim == j, gates[part * per + j], gate)
        gated_ref[:, own] = (dout_ref[:, own].astype(F32) * gate).astype(BF)
    clip = meta_ref[2:3, :]

    def step(which, carry):
        start = pl.multiple_of(which * CAP, CAP)
        slot = lax.broadcasted_iota(jnp.int32, (CAP, rows), 0)
        allowed = (slot < ranges[6 + which]) & (clip == which)
        for part in range(width // lanes):
            k_lanes = slice(part * lanes, (part + 1) * lanes)
            v_lanes = slice(width + part * lanes, width + (part + 1) * lanes)
            keys = tkv_ref[pl.ds(start, CAP), k_lanes]
            values = tkv_ref[pl.ds(start, CAP), v_lanes]
            key_grad = value_grad = 0.0
            for j in range(per):
                h = part * per + j
                own = slice(h * head_dim, (h + 1) * head_dim)
                queries = own_lanes(q_ref[:, k_lanes], j, head_dim)
                grads = own_lanes(gated_ref[:, k_lanes], j, head_dim)
                scores = dot_nt(keys, queries)
                probs = jnp.where(allowed, jnp.exp(scores - lse_ref[h : h + 1, :]), 0.0)
                prob_grad = dot_nt(values, grads)
                value_grad = value_grad + dot(probs.astype(BF), grads)
                inner = jnp.sum(probs * prob_grad, 0, keepdims=True)
                score_grad = (probs * (prob_grad - inner)).astype(BF)
                key_grad = key_grad + dot(score_grad, queries)
                product = dot_tn(keys, score_grad)[j * head_dim : (j + 1) * head_dim, :]
                acc_ref[own, :] = acc_ref[own, :] + product
            dtkv_ref[pl.ds(start, CAP), k_lanes] = key_grad.astype(dtkv_ref.dtype)
            dtkv_ref[pl.ds(start, CAP), v_lanes] = value_grad.astype(dtkv_ref.dtype)
        return carry

    lax.fori_loop(ranges[2], ranges[3], step, 0)


def self_backward_kernel(
    head_dim,
    lanes,
    own_rows,
    ranges,
    q_ref,
    kv_ref,
    meta_ref,
    dout_ref,
    self_ref,
    lse_ref,
    start_ref,
    dq_ref,
    dkv_ref,
    delta_ref,
    acc_ref,
):
    rows, width = q_ref.shape
    per = lanes // head_dim
    dkv_ref[...] = jnp.zeros(dkv_ref.shape, dkv_ref.dtype)
    acc_ref[...] = start_ref[...]
    for part in range(width // lanes):
        own = slice(part * lanes, (part + 1) * lanes)
        product = (dout_ref[:, own].astype(F32) * self_ref[:, own]).T
        for j in range(per):
            h = part * per + j
            delta_ref[h : h + 1, :] = jnp.sum(
                product[j * head_dim : (j + 1) * head_dim, :], 0, keepdims=True
            )
    first = meta_ref[0:1, :]
    last = meta_ref[1:2, :]

    def visit(start, key_index):
        allowed = (key_index >= first) & (key_index < last)
        for part in range(width // lanes):
            k_lanes = slice(part * lanes, (part + 1) * lanes)
            v_lanes = slice(width + part * lanes, width + (part + 1) * lanes)
            keys = kv_ref[pl.ds(start, KEY_BLOCK), k_lanes]
            values = kv_ref[pl.ds(start, KEY_BLOCK), v_lanes]
            key_grad = value_grad = 0.0
            for j in range(per):
                h = part * per + j
                own = slice(h * head_dim, (h + 1) * head_dim)
                queries = own_lanes(q_ref[:, k_lanes], j, head_dim)
                grads = own_lanes(dout_ref[:, k_lanes], j, head_dim)
                scores = dot_nt(keys, queries)
                probs = jnp.where(allowed, jnp.exp(scores - lse_ref[h : h + 1, :]), 0.0)
                prob_grad = dot_nt(values, grads)
                value_grad = value_grad + dot(probs.astype(BF), grads)
                score_grad = (probs * (prob_grad - delta_ref[h : h + 1, :])).astype(BF)
                key_grad = key_grad + dot(score_grad, queries)
                product = dot_tn(keys, score_grad)[j * head_dim : (j + 1) * head_dim, :]
                acc_ref[own, :] = acc_ref[own, :] + product
            dkv_ref[pl.ds(start, KEY_BLOCK), k_lanes] = key_grad.astype(BF)
            dkv_ref[pl.ds(start, KEY_BLOCK), v_lanes] = value_grad.astype(BF)

    key_blocks(ranges, own_rows, rows, visit)
    for part in range(width // lanes):
        own = slice(part * lanes, (part + 1) * lanes)
        dq_ref[:, own] = acc_ref[own, :].T * (1.0 / math.sqrt(head_dim))


SMEM = pl.BlockSpec(memory_space=pltpu.SMEM)
WHOLE = pl.BlockSpec(memory_space=pltpu.VMEM)


def join_kernel(rows, seq_ref, even_ref, odd_ref, out_ref):
    for core, source in enumerate((even_ref, odd_ref)):
        for i in range(source.shape[0] // rows):
            start = pl.multiple_of((seq_ref[0] ^ (2 * i + core)) * rows, rows)
            out_ref[pl.ds(start, rows), :] = source[i * rows : (i + 1) * rows, :]


def join_columns_kernel(rows, seq_ref, even_ref, odd_ref, out_ref):
    lanes = even_ref.shape[1]
    for core, source in enumerate((even_ref, odd_ref)):
        for i in range(source.shape[0] // rows):
            start = pl.multiple_of((seq_ref[0] ^ (2 * i + core)) * lanes, lanes)
            piece = source[i * rows : (i + 1) * rows, :]
            out_ref[:, pl.ds(start, lanes)] = piece.astype(out_ref.dtype)


def place(even, odd, seq, dim, dtype):
    chips = lax.axis_size("seq") // 2
    rows = even.shape[0] // chips
    kernel = join_kernel if dim == 0 else join_columns_kernel
    shape = (2 * even.shape[0], even.shape[1])
    if dim == 1:
        shape = (rows, 2 * chips * even.shape[1])
    return pl.pallas_call(
        functools.partial(kernel, rows),
        out_shape=jax.ShapeDtypeStruct(shape, dtype),
        in_specs=[SMEM] + [WHOLE] * 2,
        out_specs=WHOLE,
        compiler_params=pltpu.CompilerParams(vmem_limit_bytes=VMEM_BYTES),
    )(jnp.reshape(seq, (1,)).astype(jnp.int32), even, odd)


def kernel_call(kernel, outputs, scratch, smem, arrays, work):
    return pl.pallas_call(
        kernel,
        out_shape=tuple(jax.ShapeDtypeStruct(shape, dtype) for shape, dtype in outputs),
        in_specs=[SMEM] * len(smem) + [WHOLE] * len(arrays),
        out_specs=(WHOLE,) * len(outputs),
        scratch_shapes=[pltpu.VMEM(shape, dtype) for shape, dtype in scratch],
        compiler_params=pltpu.CompilerParams(vmem_limit_bytes=VMEM_BYTES),
        cost_estimate=pl.CostEstimate(
            flops=work, bytes_accessed=sum(a.size * 2 for a in arrays), transcendentals=0
        ),
    )(*smem, *arrays)


def self_forward(ranges, queries, kv, meta, head_dim, lanes, own_rows):
    rows, width = queries.shape
    return kernel_call(
        functools.partial(self_forward_kernel, head_dim, lanes, own_rows),
        [((rows, width), F32), ((8, rows), F32)],
        [((8, rows), F32), ((8, rows), F32), ((width, rows), F32)],
        [ranges],
        [queries, kv, meta],
        KERNEL_WORK * rows * kv.shape[0] * width,
    )


def cross_forward(ranges, gates, queries, tkv, meta, self_out, head_dim, lanes):
    rows, width = queries.shape
    return kernel_call(
        functools.partial(cross_forward_kernel, head_dim, lanes),
        [((rows, width), BF), ((rows, width), F32), ((8, rows), F32)],
        [((width, rows), F32)],
        [ranges, gates],
        [queries, tkv, meta, self_out],
        KERNEL_WORK * rows * CAP * width,
    )


def cross_backward(ranges, gates, queries, tkv, meta, dout, lse, head_dim, lanes):
    rows, width = queries.shape
    return kernel_call(
        functools.partial(cross_backward_kernel, head_dim, lanes),
        [((width, rows), F32), (tkv.shape, BF)],
        [((rows, width), BF)],
        [ranges, gates],
        [queries, tkv, meta, dout, lse],
        2 * KERNEL_WORK * rows * CAP * width,
    )


def self_backward(ranges, queries, kv, meta, dout, self_out, lse, start, head_dim, lanes, own_rows):
    rows, width = queries.shape
    return kernel_call(
        functools.partial(self_backward_kernel, head_dim, lanes, own_rows),
        [((rows, width), F32), (kv.shape, BF)],
        [((8, rows), F32), ((width, rows), F32)],
        [ranges],
        [queries, kv, meta, dout, self_out, lse, start],
        2 * KERNEL_WORK * rows * kv.shape[0] * width,
    )


def body(
    video,
    conditioning,
    captions,
    clip_lengths,
    cap_lengths,
    positions,
    ada_weight,
    ada_bias,
    query_weight,
    key_weight,
    value_weight,
    out_weight,
    text_key_weight,
    text_value_weight,
    gate_weight,
    up_weight,
    down_weight,
    attn_gain,
    query_gain,
    key_gain,
    text_key_gain,
    attn_out_gain,
    ffn_gain,
    ffn_out_gain,
    cross_gate,
    cotangent,
):
    num_sub = lax.axis_size("sub")
    num_seq = lax.axis_size("seq")
    rows, width = video.shape
    heads_total = cross_gate.shape[0]
    head_dim = width // heads_total
    heads = heads_total // num_sub
    cols = width // num_sub
    device = lax.axis_index(BOTH)
    seq = lax.axis_index("seq")
    sub = lax.axis_index("sub")
    group = rows * num_sub
    tokens = group * num_seq
    clips = clip_lengths.shape[0]
    clip_range = jnp.arange(clips, dtype=jnp.int32)
    score_scale = 1.0 / math.sqrt(head_dim)

    ends = jnp.cumsum(clip_lengths)
    starts = ends - clip_lengths
    member = jnp.arange(group, dtype=jnp.int32)
    group_token = (seq * num_sub + (sub ^ (member // rows))) * rows + member % rows
    group_clip = clip_index(group_token, clip_lengths)
    group_hot_bool = group_clip[:, None] == clip_range[None, :]
    group_hot = group_hot_bool.astype(F32)
    own_hot = group_hot[:rows]
    first = jnp.sum(jnp.where(group_hot_bool, starts[None, :], 0), 1)
    last = jnp.sum(jnp.where(group_hot_bool, ends[None, :], 0), 1)
    meta = jnp.concatenate(
        [first[None], last[None], group_clip[None], jnp.zeros((5, group), jnp.int32)], 0
    )
    ranges = jnp.concatenate(
        [
            jnp.stack(
                [
                    jnp.min(first) // KEY_BLOCK,
                    (jnp.max(last) + KEY_BLOCK - 1) // KEY_BLOCK,
                    jnp.min(group_clip),
                    jnp.max(group_clip) + 1,
                    seq,
                    sub,
                ]
            ).astype(jnp.int32),
            cap_lengths,
        ]
    )
    gate_tanh = jnp.tanh(cross_gate.astype(F32))
    gates = lax.dynamic_slice_in_dim(gate_tanh, sub * heads, heads, 0)

    cond_float = conditioning.astype(F32)
    cond_act = jax.nn.silu(cond_float).astype(BF)
    cond_rows = ada_weight.shape[0]
    cond_slice = lax.dynamic_slice_in_dim(cond_act, device * cond_rows, cond_rows, 1)
    mod_part = dot(cond_slice, ada_weight)
    mod_part = mod_part + lax.dynamic_update_slice_in_dim(
        jnp.zeros((1, 4 * width), F32), ada_bias.astype(F32)[None], device * ada_bias.shape[0], 1
    )
    mod_part = mod_part.reshape(clips, 4, width)
    gain_rows = attn_gain.shape[0]

    def spread(gains):
        stacked = jnp.stack(gains).astype(F32)
        return lax.dynamic_update_slice_in_dim(
            jnp.zeros((len(gains), width), F32), stacked, device * gain_rows, 1
        )

    order = Schedule()
    out_full = gather_rows(out_weight, BOTH)
    early_flow = Flow(
        total_cube(
            jnp.concatenate([mod_part[:, 0], spread([attn_gain, query_gain, key_gain])], 0),
            ("seq", "sub"),
        )
    )
    late_flow = Flow(
        total_cube(
            jnp.concatenate(
                [
                    mod_part[:, 1],
                    mod_part[:, 2],
                    mod_part[:, 3],
                    spread([text_key_gain, attn_out_gain, ffn_gain, ffn_out_gain]),
                ],
                0,
            ),
            ("seq", "sub"),
        )
    )
    w_rows = query_weight.shape[0]
    qkv_blocks = [
        jnp.concatenate(parts, 1)
        for parts in zip(*[blocks_for(w, 1) for w in (query_weight, key_weight, value_weight)])
    ]
    flow = Flow(swap_direct(qkv_blocks))
    order.step(flow, early_flow)
    packed = jnp.concatenate(
        [video, jnp.pad(positions.astype(BF), ((0, 0), (0, 128 - positions.shape[1])))], 1
    )
    packed = gather_rows(order.tie(packed)[0], "sub")
    flow = Flow(gather_seq(jnp.concatenate(in_order(flow.result, sub), 0)))
    while not (flow.done and early_flow.done):
        order.step(flow, early_flow)
    qkv_weight = flow.result
    early = early_flow.result
    scale_rows = early[:clips]
    attn_gain_f = early[clips : clips + 1]
    query_gain_f = lax.dynamic_slice_in_dim(early[clips + 1 : clips + 2], sub * cols, cols, 1)
    key_gain_f = lax.dynamic_slice_in_dim(early[clips + 2 : clips + 3], sub * cols, cols, 1)
    packed = jnp.concatenate(blocks_for(packed, 0), 0)
    video_group = packed[:, :width].astype(F32)
    group_pos = packed[:, width : width + 3].astype(F32)
    cap_shard = captions.shape[0]
    cap_total = cap_shard * num_sub
    t_rows = text_key_weight.shape[0]
    t_block = num_sub * t_rows
    cap_block = lax.dynamic_slice_in_dim(captions, seq * t_block, t_block, 1)
    cap_block = lax.optimization_barrier((cap_block, packed))[0]
    cap_block = swap_copies(cap_block).reshape(cap_total, t_block)
    text_weight = jnp.stack(
        [
            jnp.concatenate(
                [w[:, i * cols : (i + 1) * cols] for w in (text_key_weight, text_value_weight)], 1
            )
            for i in range(num_sub)
        ]
    )
    text_weight = lax.optimization_barrier((text_weight, cap_block))[0]
    text_weight = swap_blocks(text_weight, "sub").reshape(t_block, 2 * cols)

    video_inv = inv_rms(video_group)
    video_hat = video_group * video_inv
    attn_scale1 = 1.0 + pick_rows(group_hot, scale_rows)
    normed = (video_hat * (attn_gain_f * attn_scale1)).astype(BF)
    qkv_pre = dot(normed, qkv_weight)
    query_pre = qkv_pre[:, :cols]
    key_pre = qkv_pre[:, cols : 2 * cols]
    flow = Flow(
        total_rows(
            jnp.stack([jnp.sum(query_pre * query_pre, 1), jnp.sum(key_pre * key_pre, 1)])
        )
    )
    order.step(flow)
    inverse = lax.rsqrt(flow.result / width + epsilon)
    query_inv = inverse[0].reshape(group, 1)
    key_inv = inverse[1].reshape(group, 1)
    query_hat = query_pre * query_inv
    key_hat = key_pre * key_inv
    cosine, sine = rope_tables(group_pos, head_dim, heads)
    queries = (rotate(query_hat * query_gain_f, cosine, sine).astype(BF) * score_scale).astype(BF)
    keys = rotate(key_hat * key_gain_f, cosine, sine).astype(BF)
    values = qkv_pre[:, 2 * cols :].astype(BF)
    lanes = 2 * head_dim if heads % 2 == 0 else head_dim
    parts = [slice(i * lanes, (i + 1) * lanes) for i in range(cols // lanes)]
    kv = gather_rows(order.tie(jnp.concatenate([keys, values], 1))[0], "seq")

    units = gate_weight.shape[1] // num_seq
    gate_up = jnp.stack(
        [
            jnp.concatenate(
                [w[:, i * units : (i + 1) * units] for w in (gate_weight, up_weight)], 1
            )
            for i in range(num_seq)
        ]
    )
    (gate_up,) = order.tie(gate_up)
    gate_up = swap_blocks(gate_up, "seq").reshape(num_seq * w_rows, 2 * units)
    gate_up = gather_rows(lax.optimization_barrier((gate_up, kv))[0], "sub")
    gate_up = (
        gate_up.reshape(num_sub, num_seq, w_rows, 2 * units)
        .transpose(1, 0, 2, 3)
        .reshape(width, 2 * units)
    )
    down_block = lax.optimization_barrier((down_weight, text_weight))[0]
    down_block = gather_rows(down_block, "sub")

    slots = cap_total // num_seq
    text_parts = {}

    def text_chain():
        part = dot(cap_block, text_weight).astype(BF)
        pre = yield from scatter_seq(part)
        key_pre = pre[:, :cols]
        square = yield from total(jnp.sum(key_pre * key_pre, 1)[None], ("sub",))
        inv = lax.rsqrt(square / width + epsilon).reshape(slots, 1)
        text_parts["inv"], text_parts["hat"] = inv, key_pre * inv
        gain = lax.dynamic_slice_in_dim(
            late_flow.result[3 * clips : 3 * clips + 1], sub * cols, cols, 1
        )
        text_parts["gain"] = gain
        gathered = yield from gather_seq(
            jnp.concatenate([(key_pre * inv * gain).astype(BF), pre[:, cols:].astype(BF)], 1)
        )
        return gathered

    for _ in range(len(axis_bits("seq")) + len(axis_bits("sub")) - 3):
        order.step(late_flow)
    text_flow = Flow(text_chain())
    for _ in range(3):
        order.step(late_flow, text_flow)
    self_out, lse = order.step(
        text_flow,
        work=lambda *a: self_forward(ranges, *a, meta, head_dim, lanes, rows),
        args=(queries, kv),
    )
    while not (text_flow.done and late_flow.done):
        order.step(text_flow, late_flow)
    tkv = text_flow.result
    text_inv, text_hat, text_key_gain_f = (text_parts[k] for k in ("inv", "hat", "gain"))
    late = late_flow.result
    attn_gate = pick_rows(own_hot, late[:clips])
    ffn_scale = pick_rows(own_hot, late[clips : 2 * clips])
    ffn_gate = pick_rows(own_hot, late[2 * clips : 3 * clips])
    attn_out_f = late[3 * clips + 1 : 3 * clips + 2]
    ffn_gain_f = late[3 * clips + 2 : 3 * clips + 3]
    ffn_out_f = late[3 * clips + 3 : 3 * clips + 4]

    mixed_heads, cross_out, cross_lse = cross_forward(
        ranges, gates, queries, tkv, meta, self_out, head_dim, lanes
    )
    flow = Flow(swap_direct([mixed_heads[i * rows : (i + 1) * rows] for i in range(num_sub)]))
    order.step(flow)
    mixed = jnp.concatenate(in_order(flow.result, sub), 1)

    def run(flow):
        while not flow.done:
            order.step(flow)
        return flow.result

    video_own = video.astype(F32)
    projected = dot(mixed, out_full)
    proj_inv = inv_rms(projected)
    proj_hat = projected * proj_inv
    attn_tanh = jnp.tanh(attn_gate)
    hidden_state = video_own + attn_tanh * proj_hat * attn_out_f
    hidden_inv = inv_rms(hidden_state)
    hidden_hat = hidden_state * hidden_inv
    ffn_mult = ffn_gain_f * (1.0 + ffn_scale)
    ffn_in = jnp.concatenate(run(Flow(gather_even_odd((hidden_hat * ffn_mult).astype(BF)))), 0)
    half = ffn_in.shape[0] // 2
    gate_up_pre = dot(ffn_in, gate_up)
    gate_pre = gate_up_pre[:, :units]
    up_pre = gate_up_pre[:, units:]
    gate_sig = jax.nn.sigmoid(gate_pre)
    gate_act = gate_pre * gate_sig
    activated = (gate_act * up_pre).astype(BF)
    down_part = dot(activated, down_block).astype(BF)
    down_out = run(Flow(scatter_even_odd(down_part[:half], down_part[half:])))
    down_inv = inv_rms(down_out)
    down_hat = down_out * down_inv
    ffn_tanh = jnp.tanh(ffn_gate)
    block_out = (hidden_state + ffn_tanh * down_hat * ffn_out_f).astype(BF)

    grad_out = cotangent.astype(F32)
    ffn_gate_grad = grad_out * down_hat * ffn_out_f * (1.0 - ffn_tanh * ffn_tanh)
    ffn_out_gain_part = jnp.sum(grad_out * ffn_tanh * down_hat, 0)
    down_grad = norm_back(down_hat, down_inv, grad_out * ffn_tanh * ffn_out_f).astype(BF)
    down_grad = jnp.concatenate(run(Flow(gather_even_odd(down_grad))), 0)
    act_grad = dot_nt(down_grad, down_block)
    gate_grad = (act_grad * up_pre * gate_sig * (1.0 + gate_pre * (1.0 - gate_sig))).astype(BF)
    up_grad = (act_grad * gate_act).astype(BF)
    gate_up_grad = jnp.concatenate([gate_grad, up_grad], 1)
    ffn_in_part = dot_nt(gate_up_grad, gate_up).astype(BF)
    ffn_in_grad = run(Flow(scatter_even_odd(ffn_in_part[:half], ffn_in_part[half:])))
    down_weight_term = dot_tn(activated, down_grad).astype(BF)
    down_weight_grad = scatter_rows(down_weight_term, "sub").astype(F32)
    gate_up_term = dot_tn(ffn_in, gate_up_grad).astype(BF)
    gate_up_term = (
        gate_up_term.reshape(num_seq, num_sub, w_rows, 2 * units)
        .transpose(1, 0, 2, 3)
        .reshape(width, 2 * units)
    )
    gate_up_term = scatter_rows(gate_up_term, "sub").reshape(num_seq, w_rows, 2 * units)

    ffn_gain_part = jnp.sum(ffn_in_grad * hidden_hat * (1.0 + ffn_scale), 0)
    ffn_scale_grad = ffn_in_grad * hidden_hat * ffn_gain_f
    hidden_grad = grad_out + norm_back(hidden_hat, hidden_inv, ffn_in_grad * ffn_mult)
    attn_gate_grad = hidden_grad * proj_hat * attn_out_f * (1.0 - attn_tanh * attn_tanh)
    attn_out_gain_part = jnp.sum(hidden_grad * attn_tanh * proj_hat, 0)
    proj_grad = norm_back(proj_hat, proj_inv, hidden_grad * attn_tanh * attn_out_f).astype(BF)
    mixed_grad = dot_nt(proj_grad, out_full).astype(BF)
    out_weight_term = dot_tn(mixed, proj_grad).astype(BF)
    flow = Flow(swap_direct(blocks_for(mixed_grad, 1)))
    order.step(flow)
    dout = jnp.concatenate(flow.result, 0)
    cross_gate_part = jnp.sum(
        (dout.astype(F32) * cross_out).reshape(group, heads, head_dim), (0, 2)
    ) * (1.0 - gates * gates)

    def clip_sums(values):
        return dot_tn(own_hot.astype(BF), values.astype(BF))

    def at_columns(part):
        return lax.dynamic_update_slice_in_dim(
            jnp.zeros((1, width), F32), part.reshape(1, -1), sub * cols, 1
        )

    gate_row = lax.dynamic_update_slice_in_dim(
        jnp.zeros((1, width), F32), cross_gate_part.reshape(1, -1), sub * heads, 1
    )
    late_flow = Flow(
        total_cube(
            jnp.concatenate(
                [
                    clip_sums(attn_gate_grad),
                    clip_sums(ffn_scale_grad),
                    clip_sums(ffn_gate_grad),
                    attn_out_gain_part[None],
                    ffn_gain_part[None],
                    ffn_out_gain_part[None],
                    gate_row,
                ],
                0,
            ),
            ("seq", "sub"),
        )
    )
    query_start, dtkv = cross_backward(
        ranges, gates, queries, tkv, meta, dout, cross_lse, head_dim, lanes
    )
    text_flow = Flow(scatter_seq(dtkv))
    def text_back_chain():
        reduced = yield from scatter_seq(dtkv)
        low = reduced[:, :cols].astype(BF).astype(F32)
        hat_grad = low * text_key_gain_f
        inner = yield from total(jnp.sum(text_hat * hat_grad, 1)[None], ("sub",))
        text_parts["gain"] = jnp.sum(low * text_hat, 0)
        pre_grad = text_inv * (hat_grad - text_hat * (inner / width).reshape(slots, 1))
        gathered = yield from gather_seq(
            jnp.concatenate([pre_grad.astype(BF), reduced[:, cols:].astype(BF)], 1)
        )
        return gathered

    text_flow = Flow(text_back_chain())
    query_rot_grad, dkv = order.step(
        text_flow,
        late_flow,
        work=lambda *a: self_backward(ranges, a[0], a[1], meta, *a[2:], head_dim, lanes, rows),
        args=(queries, kv, dout, self_out, lse, query_start),
    )
    dkv = scatter_rows(dkv, "seq")
    out_weight_term = lax.optimization_barrier((out_weight_term, dkv))[0]
    out_weight_grad = scatter_rows(scatter_rows(out_weight_term, "seq"), "sub").astype(F32)
    while not (text_flow.done and late_flow.done):
        order.step(text_flow, late_flow)
    text_key_gain_part = text_parts["gain"]
    text_grad = text_flow.result
    query_rot_grad = query_rot_grad.astype(BF).astype(F32)
    key_rot_grad = dkv[:, :cols].astype(F32)
    value_grad = dkv[:, cols:]
    query_norm_grad = rotate(query_rot_grad, cosine, -sine)
    query_gain_part = jnp.sum(query_norm_grad * query_hat, 0)
    query_hat_grad = query_norm_grad * query_gain_f
    key_norm_grad = rotate(key_rot_grad, cosine, -sine)
    key_gain_part = jnp.sum(key_norm_grad * key_hat, 0)
    key_hat_grad = key_norm_grad * key_gain_f
    flow = Flow(
        total_rows(
            jnp.stack(
                [jnp.sum(query_hat * query_hat_grad, 1), jnp.sum(key_hat * key_hat_grad, 1)]
            )
        )
    )
    order.step(flow)
    inner = flow.result / width
    caption_part = dot_nt(text_grad, text_weight).astype(BF).reshape(num_sub, cap_shard, t_block)
    text_term = dot_tn(cap_block, text_grad).astype(BF).reshape(num_sub, t_rows, 2 * cols)
    query_pre_grad = query_inv * (query_hat_grad - query_hat * inner[0].reshape(group, 1))
    key_pre_grad = key_inv * (key_hat_grad - key_hat * inner[1].reshape(group, 1))
    qkv_grad = jnp.concatenate([query_pre_grad.astype(BF), key_pre_grad.astype(BF), value_grad], 1)
    qkv_term = dot_tn(normed, qkv_grad).astype(BF)
    normed_part = dot_nt(qkv_grad, qkv_weight)

    hat_grad = normed_part * video_hat
    attn_gain_part = jnp.sum(hat_grad * attn_scale1, 0)
    scale_part = dot_tn(group_hot.astype(BF), (hat_grad * attn_gain_f).astype(BF))
    early_flow = Flow(
        total(
            jnp.concatenate(
                [
                    scale_part,
                    attn_gain_part[None],
                    at_columns(query_gain_part),
                    at_columns(key_gain_part),
                    at_columns(text_key_gain_part),
                ],
                0,
            ),
            ("seq", "sub"),
        )
    )
    qkv_flow = Flow(scatter_seq(qkv_term))
    caption_block = jnp.sum(
        swap_blocks(order.tie(caption_part)[0], "sub").astype(F32), 0
    ).astype(BF)
    normed_low = jnp.concatenate(blocks_for(normed_part.astype(BF), 0), 0)
    normed_grad = scatter_rows(order.tie(normed_low)[0], "sub").astype(F32)
    text_term = lax.optimization_barrier((text_term, normed_grad))[0]
    text_term = swap_blocks(text_term, "sub")
    caption_flow = Flow(gather_seq(caption_block, 1, F32))
    order.step(early_flow, qkv_flow)
    order.step(early_flow, qkv_flow)
    order.step(early_flow)
    late_sum = late_flow.result
    early_sum = early_flow.result
    mod_low = jnp.concatenate(
        [
            early_sum[:clips],
            late_sum[:clips],
            late_sum[clips : 2 * clips],
            late_sum[2 * clips : 3 * clips],
        ],
        1,
    ).astype(BF)
    cond_part = lax.dynamic_update_slice_in_dim(
        jnp.zeros(conditioning.shape, F32), dot_nt(mod_low, ada_weight), device * cond_rows, 1
    )
    cond_flow = Flow(total(cond_part, ("seq", "sub")))
    qkv_term = order.tie(qkv_flow.result.astype(BF).reshape(num_sub, w_rows, 3 * cols))[0]
    qkv_term = swap_blocks(qkv_term, "sub")
    order.step(caption_flow)
    order.step(cond_flow, caption_flow)
    order.step(cond_flow)
    order.step(cond_flow)
    caption_grad = caption_flow.result
    query_weight_grad, key_weight_grad, value_weight_grad = (
        jnp.concatenate([block[:, j * cols : (j + 1) * cols] for block in qkv_term], 1).astype(F32)
        for j in range(3)
    )
    text_key_weight_grad, text_value_weight_grad = (
        jnp.concatenate([block[:, j * cols : (j + 1) * cols] for block in text_term], 1).astype(F32)
        for j in range(2)
    )
    gate_up_term = swap_blocks(gate_up_term, "seq")
    gate_weight_grad, up_weight_grad = (
        jnp.concatenate(
            [gate_up_term[i, :, j * units : (j + 1) * units] for i in range(num_seq)], 1
        ).astype(F32)
        for j in range(2)
    )

    own_hat, own_inv, own_scale1 = video_hat[:rows], video_inv[:rows], attn_scale1[:rows]
    video_grad = hidden_grad + norm_back(own_hat, own_inv, normed_grad * (attn_gain_f * own_scale1))

    def own_gain(row):
        return lax.dynamic_slice_in_dim(row, device * gain_rows, gain_rows, 0)

    bias_rows = ada_bias.shape[0]
    ada_bias_grad = jnp.sum(
        lax.dynamic_slice_in_dim(mod_low.astype(F32), device * bias_rows, bias_rows, 1), 0
    )
    ada_weight_grad = dot_tn(cond_slice, mod_low)
    cond_sig = jax.nn.sigmoid(cond_float)
    cond_grad = cond_flow.result * cond_sig * (1.0 + cond_float * (1.0 - cond_sig))
    return (
        block_out,
        video_grad,
        caption_grad,
        cond_grad,
        ada_weight_grad,
        ada_bias_grad,
        query_weight_grad,
        key_weight_grad,
        value_weight_grad,
        out_weight_grad,
        text_key_weight_grad,
        text_value_weight_grad,
        gate_weight_grad,
        up_weight_grad,
        down_weight_grad,
        own_gain(early_sum[clips]),
        own_gain(early_sum[clips + 1]),
        own_gain(early_sum[clips + 2]),
        own_gain(early_sum[clips + 3]),
        own_gain(late_sum[3 * clips]),
        own_gain(late_sum[3 * clips + 1]),
        own_gain(late_sum[3 * clips + 2]),
        late_sum[3 * clips + 3, :heads_total],
    )


def solution(mesh):
    matrix = P(BOTH, None)
    vector = P(BOTH)
    return jax.shard_map(
        body,
        mesh=mesh,
        in_specs=(matrix, P(), P("sub", None), P(), P(), matrix, matrix, vector)
        + (matrix,) * 9
        + (vector,) * 7
        + (P(), matrix),
        out_specs=(matrix, matrix, P("sub", None), P(), matrix, vector)
        + (matrix,) * 9
        + (vector,) * 7
        + (P(),),
        check_vma=False,
    )
```

```python
import functools
import math

import jax
import jax.numpy as jnp
import numpy as np
from jax import lax
from jax.experimental import pallas as pl
from jax.experimental.pallas import tpu as pltpu
from jax.sharding import PartitionSpec as P

CAP = 256
KEY_BLOCK = 512
epsilon = 1e-06
rope_base = 10000.0
masked_score = -1e30
BF = jnp.bfloat16
F32 = jnp.float32
BOTH = ("seq", "sub")
VMEM_BYTES = 56 * 1024 * 1024
KERNEL_WORK = 16


def axis_bits(axis):
    masks, mask = [], 1
    while mask < lax.axis_size(axis):
        masks.append(mask)
        mask *= 2
    return masks


def send(values, axis, mask):
    count = lax.axis_size(axis)
    return lax.ppermute(values, axis, [(i, i ^ mask) for i in range(count)])


class Flow:
    def __init__(self, stages):
        self.stages = stages
        self.result = None
        self.done = False
        self.wanted = next(stages)

    def feed(self, arrived):
        try:
            self.wanted = self.stages.send(arrived)
        except StopIteration as stop:
            self.wanted, self.done, self.result = [], True, stop.value


class Schedule:
    def __init__(self):
        self.frontier = ()

    def tie(self, *arrays):
        tied = lax.optimization_barrier(tuple(arrays) + self.frontier)
        return tied[: len(arrays)]

    def step(self, *flows, work=None, args=()):
        flows = [flow for flow in flows if not flow.done]
        sends = [item for flow in flows for item in flow.wanted]
        tied = self.tie(*[item[0] for item in sends], *args)
        arrived = [send(value, item[1], item[2]) for value, item in zip(tied, sends)]
        outputs = work(*tied[len(sends) :]) if work is not None else ()
        self.frontier = tuple(arrived) + tuple(jax.tree.leaves(outputs))
        for flow in flows:
            count = len(flow.wanted)
            flow.feed(arrived[:count])
            arrived = arrived[count:]
        return outputs

    def start(self, flow, *others):
        tied = lax.optimization_barrier(
            tuple(item[0] for item in flow.wanted) + self.frontier + tuple(others)
        )
        flow.feed([send(v, item[1], item[2]) for v, item in zip(tied, flow.wanted)])
        return flow.result

    def held(self, values):
        return list(self.tie(*values))


def in_order(pieces, index):
    mask = 1
    while mask < len(pieces):
        flip = (index // mask) % 2 == 1
        pieces = [jnp.where(flip, pieces[i ^ mask], pieces[i]) for i in range(len(pieces))]
        mask *= 2
    return pieces


def rows_in_order(pieces, index):
    shape = pieces[0][1].shape
    result = jnp.zeros((len(pieces),) + shape, pieces[0][1].dtype)
    for mask, piece in pieces:
        result = lax.dynamic_update_index_in_dim(result, piece, index ^ mask, 0)
    return result.reshape((len(pieces) * shape[0],) + shape[1:])


def gather_even_odd(values, axis="seq"):
    arrived = yield [(values, axis, mask) for mask in range(2, lax.axis_size(axis), 2)]
    even = jnp.concatenate([values] + arrived, 0)
    (odd,) = yield [(even, axis, 1)]
    return even, odd


def scatter_even_odd(even, odd, axis="seq"):
    count = lax.axis_size(axis) // 2
    rows = even.shape[0] // count
    (other,) = yield [(odd, axis, 1)]
    held = (even.astype(F32) + other.astype(F32)).astype(even.dtype)
    arrived = yield [
        (held[i * rows : (i + 1) * rows], axis, 2 * i) for i in range(1, count)
    ]
    result = held[:rows].astype(F32)
    for piece in arrived:
        result = result + piece.astype(F32)
    return result


def gather_seq(values, dim=0, dtype=None):
    even, odd = yield from gather_even_odd(values)
    return place(even, odd, lax.axis_index("seq"), dim, dtype or values.dtype)


def scatter_seq(values):
    index = lax.axis_index("seq")
    count = lax.axis_size("seq")
    blocks = values.reshape((count, values.shape[0] // count) + values.shape[1:])
    halves = [
        jnp.concatenate(
            [
                lax.dynamic_index_in_dim(blocks, index ^ mask, 0, keepdims=False)
                for mask in range(core, count, 2)
            ],
            0,
        )
        for core in range(2)
    ]
    result = yield from scatter_even_odd(*halves)
    return result


def pair_sum(pieces):
    while len(pieces) > 1:
        pieces = [pieces[i] + pieces[i + 1] for i in range(0, len(pieces), 2)]
    return pieces[0]


def total(values, axes):
    for axis in axes:
        groups = [range(1, lax.axis_size(axis))]
        if axis == "seq":
            groups = [range(2, lax.axis_size(axis), 2), [1]]
        for masks in groups:
            arrived = yield [(values, axis, mask) for mask in masks]
            values = pair_sum([values] + arrived)
    return values


def total_cube(values, axes):
    for axis in axes:
        for mask in axis_bits(axis):
            (other,) = yield [(values, axis, mask)]
            values = values + other
    return values


def total_rows(values, axis="sub"):
    count = lax.axis_size(axis)
    rows = values.shape[1] // count
    arrived = yield [(values, axis, mask) for mask in range(1, count)]
    for mask, other in enumerate(arrived, 1):
        values = values + jnp.concatenate(
            [other[:, (i ^ mask) * rows : ((i ^ mask) + 1) * rows] for i in range(count)], 1
        )
    return values


def gather_direct(values, axis="sub"):
    arrived = yield [(values, axis, mask) for mask in range(1, lax.axis_size(axis))]
    return [values] + arrived


def swap_direct(blocks, axis="sub"):
    arrived = yield [(blocks[mask], axis, mask) for mask in range(1, len(blocks))]
    return [blocks[0]] + arrived


def scatter_direct(blocks, axis="sub"):
    arrived = yield [(blocks[mask], axis, mask) for mask in range(1, len(blocks))]
    result = blocks[0].astype(F32)
    for other in arrived:
        result = result + other.astype(F32)
    return result


def blocks_for(values, dim, axis="sub"):
    index = lax.axis_index(axis)
    count = lax.axis_size(axis)
    size = values.shape[dim] // count
    if dim == 0:
        blocks = values.reshape((count, size) + values.shape[1:])
        return [
            lax.dynamic_index_in_dim(blocks, index ^ mask, 0, keepdims=False)
            for mask in range(count)
        ]
    return in_order([values[:, i * size : (i + 1) * size] for i in range(count)], index)


def swap_blocks(values, axis):
    return lax.all_to_all(values, axis, split_axis=0, concat_axis=0, tiled=True)


def swap_copies(values, axis="sub"):
    return swap_blocks(jnp.broadcast_to(values[None], (lax.axis_size(axis),) + values.shape), axis)


def gather_rows(values, axis):
    return lax.all_gather(values, axis, axis=0, tiled=True)


def scatter_rows(values, axis):
    return lax.psum_scatter(values, axis, scatter_dimension=0, tiled=True)


def inv_rms(values):
    return lax.rsqrt(jnp.mean(values * values, -1, keepdims=True) + epsilon)


def norm_back(normed_hat, inverse, grad_hat):
    return inverse * (grad_hat - normed_hat * jnp.mean(normed_hat * grad_hat, -1, keepdims=True))


def dot(left, right):
    return jnp.dot(left, right, preferred_element_type=F32)


def dot_nt(left, right):
    return lax.dot_general(left, right, (((1,), (1,)), ((), ())), preferred_element_type=F32)


def dot_tn(left, right):
    return lax.dot_general(left, right, (((0,), (0,)), ((), ())), preferred_element_type=F32)


def rope_tables(positions, head_dim, heads):
    pair_total = head_dim // 2
    frame_pairs = pair_total // 4
    height_pairs = (pair_total - frame_pairs) // 2
    width_pairs = pair_total - frame_pairs - height_pairs
    frequency = np.zeros((3, pair_total), np.float32)
    start = 0
    for axis_id, pair_count in enumerate((frame_pairs, height_pairs, width_pairs)):
        exponent = -np.arange(pair_count, dtype=np.float32) / np.float32(pair_count)
        frequency[axis_id, start : start + pair_count] = np.float32(rope_base) ** exponent
        start += pair_count
    frequency = jnp.asarray(np.repeat(frequency, 2, axis=1))
    angles = (
        positions[:, 0:1] * frequency[0:1]
        + positions[:, 1:2] * frequency[1:2]
        + positions[:, 2:3] * frequency[2:3]
    )
    sign = jnp.asarray(np.where(np.arange(head_dim) % 2 == 0, -1.0, 1.0).astype(np.float32))
    cosine = jnp.cos(angles)
    sine = jnp.sin(angles) * sign[None, :]
    return (jnp.tile(cosine, (1, heads)), jnp.tile(sine, (1, heads)))


def rotate(values, cosine, sine):
    even = lax.broadcasted_iota(jnp.int32, values.shape, 1) % 2 == 0
    swapped = jnp.where(even, jnp.roll(values, -1, 1), jnp.roll(values, 1, 1))
    return values * cosine + swapped * sine


def clip_index(token_index, clip_lengths):
    bounds = jnp.cumsum(clip_lengths)
    return jnp.sum((token_index[:, None] >= bounds[None, :]).astype(jnp.int32), 1)


def pick_rows(onehot, rows):
    picked = onehot[:, 0:1] * rows[0:1]
    for clip in range(1, rows.shape[0]):
        picked = picked + onehot[:, clip : clip + 1] * rows[clip : clip + 1]
    return picked


def own_lanes(block, head, head_dim):
    if block.shape[1] == head_dim:
        return block
    lane = lax.broadcasted_iota(jnp.int32, block.shape, 1)
    return jnp.where(lane // head_dim == head, block, jnp.zeros_like(block))


def key_blocks(ranges, own_rows, rows, visit):
    per_group = rows // KEY_BLOCK
    per_block = KEY_BLOCK // own_rows

    def step(place, carry):
        block = (place // per_group) * per_group
        block = block + ((place % per_group) ^ (ranges[5] // per_block))
        row = lax.broadcasted_iota(jnp.int32, (KEY_BLOCK, rows), 0)
        index = place * KEY_BLOCK + (row ^ ((ranges[5] % per_block) * own_rows))
        visit(pl.multiple_of(block * KEY_BLOCK, KEY_BLOCK), index)
        return carry

    lax.fori_loop(ranges[0], ranges[1], step, 0)


def self_forward_kernel(
    head_dim,
    lanes,
    own_rows,
    ranges,
    q_ref,
    kv_ref,
    meta_ref,
    self_ref,
    lse_ref,
    max_ref,
    sum_ref,
    acc_ref,
):
    rows, width = q_ref.shape
    per = lanes // head_dim
    max_ref[...] = jnp.full(max_ref.shape, masked_score, F32)
    sum_ref[...] = jnp.zeros(sum_ref.shape, F32)
    acc_ref[...] = jnp.zeros(acc_ref.shape, F32)
    first = meta_ref[0:1, :]
    last = meta_ref[1:2, :]

    def visit(start, key_index):
        allowed = (key_index >= first) & (key_index < last)
        for part in range(width // lanes):
            k_lanes = slice(part * lanes, (part + 1) * lanes)
            keys = kv_ref[pl.ds(start, KEY_BLOCK), k_lanes]
            values = kv_ref[pl.ds(start, KEY_BLOCK), width + part * lanes : width + (part + 1) * lanes]
            for j in range(per):
                h = part * per + j
                own = slice(h * head_dim, (h + 1) * head_dim)
                queries = own_lanes(q_ref[:, k_lanes], j, head_dim)
                scores = jnp.where(allowed, dot_nt(keys, queries), masked_score)
                old_max = max_ref[h : h + 1, :]
                new_max = jnp.maximum(old_max, jnp.max(scores, 0, keepdims=True))
                probs = jnp.exp(scores - new_max)
                factor = jnp.exp(old_max - new_max)
                max_ref[h : h + 1, :] = new_max
                sum_ref[h : h + 1, :] = sum_ref[h : h + 1, :] * factor + jnp.sum(
                    probs, 0, keepdims=True
                )
                product = dot_tn(values, probs.astype(BF))[j * head_dim : (j + 1) * head_dim, :]
                acc_ref[own, :] = acc_ref[own, :] * factor + product

    key_blocks(ranges, own_rows, rows, visit)
    lse_ref[...] = jnp.zeros(lse_ref.shape, F32)
    for h in range(width // head_dim):
        own = slice(h * head_dim, (h + 1) * head_dim)
        sums = sum_ref[h : h + 1, :]
        acc_ref[own, :] = acc_ref[own, :] / sums
        lse_ref[h : h + 1, :] = max_ref[h : h + 1, :] + jnp.log(sums)
    for part in range(width // lanes):
        own = slice(part * lanes, (part + 1) * lanes)
        self_ref[:, own] = acc_ref[own, :].T


def cross_forward_kernel(
    head_dim, lanes, ranges, gates, q_ref, tkv_ref, meta_ref, self_ref, mixed_ref, cross_ref, lse_ref, acc_ref
):
    rows, width = q_ref.shape
    acc_ref[...] = jnp.zeros(acc_ref.shape, F32)
    lse_ref[...] = jnp.zeros(lse_ref.shape, F32)
    clip = meta_ref[2:3, :]
    per = lanes // head_dim

    def step(which, carry):
        start = pl.multiple_of(which * CAP, CAP)
        slot = lax.broadcasted_iota(jnp.int32, (CAP, rows), 0)
        valid = slot < ranges[6 + which]
        here = clip == which
        for part in range(width // lanes):
            keys = tkv_ref[pl.ds(start, CAP), part * lanes : (part + 1) * lanes]
            values = tkv_ref[pl.ds(start, CAP), width + part * lanes : width + (part + 1) * lanes]
            queries = q_ref[:, part * lanes : (part + 1) * lanes]
            for j in range(per):
                h = part * per + j
                own = slice(h * head_dim, (h + 1) * head_dim)
                scores = dot_nt(keys, own_lanes(queries, j, head_dim))
                scores = jnp.where(valid, scores, masked_score)
                top = jnp.max(scores, 0, keepdims=True)
                probs = jnp.exp(scores - top)
                sums = jnp.sum(probs, 0, keepdims=True)
                probs = (probs / sums).astype(BF)
                product = dot_tn(values, probs)[j * head_dim : (j + 1) * head_dim, :]
                acc_ref[own, :] = jnp.where(here, product, acc_ref[own, :])
                lse_ref[h : h + 1, :] = jnp.where(here, top + jnp.log(sums), lse_ref[h : h + 1, :])
        return carry

    lax.fori_loop(ranges[2], ranges[3], step, 0)
    lane = lax.broadcasted_iota(jnp.int32, (1, lanes), 1)
    for part in range(width // lanes):
        own = slice(part * lanes, (part + 1) * lanes)
        cross = acc_ref[own, :].T
        gate = jnp.full((1, lanes), gates[part * per], F32)
        for j in range(1, per):
            gate = jnp.where(lane // head_dim == j, gates[part * per + j], gate)
        cross_ref[:, own] = cross
        mixed_ref[:, own] = (self_ref[:, own].astype(BF).astype(F32) + gate * cross).astype(BF)


def cross_backward_kernel(
    head_dim, lanes, ranges, gates, q_ref, tkv_ref, meta_ref, dout_ref, lse_ref, acc_ref, dtkv_ref, gated_ref
):
    rows, width = q_ref.shape
    per = lanes // head_dim
    dtkv_ref[...] = jnp.zeros(dtkv_ref.shape, dtkv_ref.dtype)
    acc_ref[...] = jnp.zeros(acc_ref.shape, F32)
    lane = lax.broadcasted_iota(jnp.int32, (1, lanes), 1)
    for part in range(width // lanes):
        own = slice(part * lanes, (part + 1) * lanes)
        gate = jnp.full((1, lanes), gates[part * per], F32)
        for j in range(1, per):
            gate = jnp.where(lane // head_dim == j, gates[part * per + j], gate)
        gated_ref[:, own] = (dout_ref[:, own].astype(F32) * gate).astype(BF)
    clip = meta_ref[2:3, :]

    def step(which, carry):
        start = pl.multiple_of(which * CAP, CAP)
        slot = lax.broadcasted_iota(jnp.int32, (CAP, rows), 0)
        allowed = (slot < ranges[6 + which]) & (clip == which)
        for part in range(width // lanes):
            k_lanes = slice(part * lanes, (part + 1) * lanes)
            v_lanes = slice(width + part * lanes, width + (part + 1) * lanes)
            keys = tkv_ref[pl.ds(start, CAP), k_lanes]
            values = tkv_ref[pl.ds(start, CAP), v_lanes]
            key_grad = value_grad = 0.0
            for j in range(per):
                h = part * per + j
                own = slice(h * head_dim, (h + 1) * head_dim)
                queries = own_lanes(q_ref[:, k_lanes], j, head_dim)
                grads = own_lanes(gated_ref[:, k_lanes], j, head_dim)
                scores = dot_nt(keys, queries)
                probs = jnp.where(allowed, jnp.exp(scores - lse_ref[h : h + 1, :]), 0.0)
                prob_grad = dot_nt(values, grads)
                value_grad = value_grad + dot(probs.astype(BF), grads)
                inner = jnp.sum(probs * prob_grad, 0, keepdims=True)
                score_grad = (probs * (prob_grad - inner)).astype(BF)
                key_grad = key_grad + dot(score_grad, queries)
                product = dot_tn(keys, score_grad)[j * head_dim : (j + 1) * head_dim, :]
                acc_ref[own, :] = acc_ref[own, :] + product
            dtkv_ref[pl.ds(start, CAP), k_lanes] = key_grad.astype(dtkv_ref.dtype)
            dtkv_ref[pl.ds(start, CAP), v_lanes] = value_grad.astype(dtkv_ref.dtype)
        return carry

    lax.fori_loop(ranges[2], ranges[3], step, 0)


def self_backward_kernel(
    head_dim,
    lanes,
    own_rows,
    ranges,
    q_ref,
    kv_ref,
    meta_ref,
    dout_ref,
    self_ref,
    lse_ref,
    start_ref,
    dq_ref,
    dkv_ref,
    delta_ref,
    acc_ref,
):
    rows, width = q_ref.shape
    per = lanes // head_dim
    dkv_ref[...] = jnp.zeros(dkv_ref.shape, dkv_ref.dtype)
    acc_ref[...] = start_ref[...]
    for part in range(width // lanes):
        own = slice(part * lanes, (part + 1) * lanes)
        product = (dout_ref[:, own].astype(F32) * self_ref[:, own]).T
        for j in range(per):
            h = part * per + j
            delta_ref[h : h + 1, :] = jnp.sum(
                product[j * head_dim : (j + 1) * head_dim, :], 0, keepdims=True
            )
    first = meta_ref[0:1, :]
    last = meta_ref[1:2, :]

    def visit(start, key_index):
        allowed = (key_index >= first) & (key_index < last)
        for part in range(width // lanes):
            k_lanes = slice(part * lanes, (part + 1) * lanes)
            v_lanes = slice(width + part * lanes, width + (part + 1) * lanes)
            keys = kv_ref[pl.ds(start, KEY_BLOCK), k_lanes]
            values = kv_ref[pl.ds(start, KEY_BLOCK), v_lanes]
            key_grad = value_grad = 0.0
            for j in range(per):
                h = part * per + j
                own = slice(h * head_dim, (h + 1) * head_dim)
                queries = own_lanes(q_ref[:, k_lanes], j, head_dim)
                grads = own_lanes(dout_ref[:, k_lanes], j, head_dim)
                scores = dot_nt(keys, queries)
                probs = jnp.where(allowed, jnp.exp(scores - lse_ref[h : h + 1, :]), 0.0)
                prob_grad = dot_nt(values, grads)
                value_grad = value_grad + dot(probs.astype(BF), grads)
                score_grad = (probs * (prob_grad - delta_ref[h : h + 1, :])).astype(BF)
                key_grad = key_grad + dot(score_grad, queries)
                product = dot_tn(keys, score_grad)[j * head_dim : (j + 1) * head_dim, :]
                acc_ref[own, :] = acc_ref[own, :] + product
            dkv_ref[pl.ds(start, KEY_BLOCK), k_lanes] = key_grad.astype(BF)
            dkv_ref[pl.ds(start, KEY_BLOCK), v_lanes] = value_grad.astype(BF)

    key_blocks(ranges, own_rows, rows, visit)
    for part in range(width // lanes):
        own = slice(part * lanes, (part + 1) * lanes)
        dq_ref[:, own] = acc_ref[own, :].T * (1.0 / math.sqrt(head_dim))


SMEM = pl.BlockSpec(memory_space=pltpu.SMEM)
WHOLE = pl.BlockSpec(memory_space=pltpu.VMEM)


def join_kernel(rows, seq_ref, even_ref, odd_ref, out_ref):
    for core, source in enumerate((even_ref, odd_ref)):
        for i in range(source.shape[0] // rows):
            start = pl.multiple_of((seq_ref[0] ^ (2 * i + core)) * rows, rows)
            out_ref[pl.ds(start, rows), :] = source[i * rows : (i + 1) * rows, :]


def join_columns_kernel(rows, seq_ref, even_ref, odd_ref, out_ref):
    lanes = even_ref.shape[1]
    for core, source in enumerate((even_ref, odd_ref)):
        for i in range(source.shape[0] // rows):
            start = pl.multiple_of((seq_ref[0] ^ (2 * i + core)) * lanes, lanes)
            piece = source[i * rows : (i + 1) * rows, :]
            out_ref[:, pl.ds(start, lanes)] = piece.astype(out_ref.dtype)


def place(even, odd, seq, dim, dtype):
    chips = lax.axis_size("seq") // 2
    rows = even.shape[0] // chips
    kernel = join_kernel if dim == 0 else join_columns_kernel
    shape = (2 * even.shape[0], even.shape[1])
    if dim == 1:
        shape = (rows, 2 * chips * even.shape[1])
    return pl.pallas_call(
        functools.partial(kernel, rows),
        out_shape=jax.ShapeDtypeStruct(shape, dtype),
        in_specs=[SMEM] + [WHOLE] * 2,
        out_specs=WHOLE,
        compiler_params=pltpu.CompilerParams(vmem_limit_bytes=VMEM_BYTES),
    )(jnp.reshape(seq, (1,)).astype(jnp.int32), even, odd)


def kernel_call(kernel, outputs, scratch, smem, arrays, work):
    return pl.pallas_call(
        kernel,
        out_shape=tuple(jax.ShapeDtypeStruct(shape, dtype) for shape, dtype in outputs),
        in_specs=[SMEM] * len(smem) + [WHOLE] * len(arrays),
        out_specs=(WHOLE,) * len(outputs),
        scratch_shapes=[pltpu.VMEM(shape, dtype) for shape, dtype in scratch],
        compiler_params=pltpu.CompilerParams(vmem_limit_bytes=VMEM_BYTES),
        cost_estimate=pl.CostEstimate(
            flops=work, bytes_accessed=sum(a.size * 2 for a in arrays), transcendentals=0
        ),
    )(*smem, *arrays)


def self_forward(ranges, queries, kv, meta, head_dim, lanes, own_rows):
    rows, width = queries.shape
    return kernel_call(
        functools.partial(self_forward_kernel, head_dim, lanes, own_rows),
        [((rows, width), F32), ((8, rows), F32)],
        [((8, rows), F32), ((8, rows), F32), ((width, rows), F32)],
        [ranges],
        [queries, kv, meta],
        KERNEL_WORK * rows * kv.shape[0] * width,
    )


def cross_forward(ranges, gates, queries, tkv, meta, self_out, head_dim, lanes):
    rows, width = queries.shape
    return kernel_call(
        functools.partial(cross_forward_kernel, head_dim, lanes),
        [((rows, width), BF), ((rows, width), F32), ((8, rows), F32)],
        [((width, rows), F32)],
        [ranges, gates],
        [queries, tkv, meta, self_out],
        KERNEL_WORK * rows * CAP * width,
    )


def cross_backward(ranges, gates, queries, tkv, meta, dout, lse, head_dim, lanes):
    rows, width = queries.shape
    return kernel_call(
        functools.partial(cross_backward_kernel, head_dim, lanes),
        [((width, rows), F32), (tkv.shape, BF)],
        [((rows, width), BF)],
        [ranges, gates],
        [queries, tkv, meta, dout, lse],
        2 * KERNEL_WORK * rows * CAP * width,
    )


def self_backward(ranges, queries, kv, meta, dout, self_out, lse, start, head_dim, lanes, own_rows):
    rows, width = queries.shape
    return kernel_call(
        functools.partial(self_backward_kernel, head_dim, lanes, own_rows),
        [((rows, width), F32), (kv.shape, BF)],
        [((8, rows), F32), ((width, rows), F32)],
        [ranges],
        [queries, kv, meta, dout, self_out, lse, start],
        2 * KERNEL_WORK * rows * kv.shape[0] * width,
    )


def body(
    video,
    conditioning,
    captions,
    clip_lengths,
    cap_lengths,
    positions,
    ada_weight,
    ada_bias,
    query_weight,
    key_weight,
    value_weight,
    out_weight,
    text_key_weight,
    text_value_weight,
    gate_weight,
    up_weight,
    down_weight,
    attn_gain,
    query_gain,
    key_gain,
    text_key_gain,
    attn_out_gain,
    ffn_gain,
    ffn_out_gain,
    cross_gate,
    cotangent,
):
    num_sub = lax.axis_size("sub")
    num_seq = lax.axis_size("seq")
    rows, width = video.shape
    heads_total = cross_gate.shape[0]
    head_dim = width // heads_total
    heads = heads_total // num_sub
    cols = width // num_sub
    device = lax.axis_index(BOTH)
    seq = lax.axis_index("seq")
    sub = lax.axis_index("sub")
    group = rows * num_sub
    tokens = group * num_seq
    clips = clip_lengths.shape[0]
    clip_range = jnp.arange(clips, dtype=jnp.int32)
    score_scale = 1.0 / math.sqrt(head_dim)

    ends = jnp.cumsum(clip_lengths)
    starts = ends - clip_lengths
    member = jnp.arange(group, dtype=jnp.int32)
    group_token = (seq * num_sub + (sub ^ (member // rows))) * rows + member % rows
    group_clip = clip_index(group_token, clip_lengths)
    group_hot_bool = group_clip[:, None] == clip_range[None, :]
    group_hot = group_hot_bool.astype(F32)
    own_hot = group_hot[:rows]
    first = jnp.sum(jnp.where(group_hot_bool, starts[None, :], 0), 1)
    last = jnp.sum(jnp.where(group_hot_bool, ends[None, :], 0), 1)
    meta = jnp.concatenate(
        [first[None], last[None], group_clip[None], jnp.zeros((5, group), jnp.int32)], 0
    )
    ranges = jnp.concatenate(
        [
            jnp.stack(
                [
                    jnp.min(first) // KEY_BLOCK,
                    (jnp.max(last) + KEY_BLOCK - 1) // KEY_BLOCK,
                    jnp.min(group_clip),
                    jnp.max(group_clip) + 1,
                    seq,
                    sub,
                ]
            ).astype(jnp.int32),
            cap_lengths,
        ]
    )
    gate_tanh = jnp.tanh(cross_gate.astype(F32))
    gates = lax.dynamic_slice_in_dim(gate_tanh, sub * heads, heads, 0)

    cond_float = conditioning.astype(F32)
    cond_act = jax.nn.silu(cond_float).astype(BF)
    cond_rows = ada_weight.shape[0]
    cond_slice = lax.dynamic_slice_in_dim(cond_act, device * cond_rows, cond_rows, 1)
    mod_part = dot(cond_slice, ada_weight)
    mod_part = mod_part + lax.dynamic_update_slice_in_dim(
        jnp.zeros((1, 4 * width), F32), ada_bias.astype(F32)[None], device * ada_bias.shape[0], 1
    )
    mod_part = mod_part.reshape(clips, 4, width)
    gain_rows = attn_gain.shape[0]

    def spread(gains):
        stacked = jnp.stack(gains).astype(F32)
        return lax.dynamic_update_slice_in_dim(
            jnp.zeros((len(gains), width), F32), stacked, device * gain_rows, 1
        )

    order = Schedule()
    out_full = gather_rows(out_weight, BOTH)
    early_flow = Flow(
        total_cube(
            jnp.concatenate([mod_part[:, 0], spread([attn_gain, query_gain, key_gain])], 0),
            ("seq", "sub"),
        )
    )
    late_flow = Flow(
        total_cube(
            jnp.concatenate(
                [
                    mod_part[:, 1],
                    mod_part[:, 2],
                    mod_part[:, 3],
                    spread([text_key_gain, attn_out_gain, ffn_gain, ffn_out_gain]),
                ],
                0,
            ),
            ("seq", "sub"),
        )
    )
    w_rows = query_weight.shape[0]
    qkv_blocks = [
        jnp.concatenate(parts, 1)
        for parts in zip(*[blocks_for(w, 1) for w in (query_weight, key_weight, value_weight)])
    ]
    flow = Flow(swap_direct(qkv_blocks))
    order.step(flow, early_flow)
    packed = jnp.concatenate(
        [video, jnp.pad(positions.astype(BF), ((0, 0), (0, 128 - positions.shape[1])))], 1
    )
    packed = gather_rows(order.tie(packed)[0], "sub")
    flow = Flow(gather_seq(jnp.concatenate(in_order(flow.result, sub), 0)))
    while not (flow.done and early_flow.done):
        order.step(flow, early_flow)
    qkv_weight = flow.result
    early = early_flow.result
    scale_rows = early[:clips]
    attn_gain_f = early[clips : clips + 1]
    query_gain_f = lax.dynamic_slice_in_dim(early[clips + 1 : clips + 2], sub * cols, cols, 1)
    key_gain_f = lax.dynamic_slice_in_dim(early[clips + 2 : clips + 3], sub * cols, cols, 1)
    packed = jnp.concatenate(blocks_for(packed, 0), 0)
    video_group = packed[:, :width].astype(F32)
    group_pos = packed[:, width : width + 3].astype(F32)
    cap_shard = captions.shape[0]
    cap_total = cap_shard * num_sub
    t_rows = text_key_weight.shape[0]
    t_block = num_sub * t_rows
    cap_block = lax.dynamic_slice_in_dim(captions, seq * t_block, t_block, 1)
    cap_block = lax.optimization_barrier((cap_block, packed))[0]
    cap_block = swap_copies(cap_block).reshape(cap_total, t_block)
    text_weight = jnp.stack(
        [
            jnp.concatenate(
                [w[:, i * cols : (i + 1) * cols] for w in (text_key_weight, text_value_weight)], 1
            )
            for i in range(num_sub)
        ]
    )
    text_weight = lax.optimization_barrier((text_weight, cap_block))[0]
    text_weight = swap_blocks(text_weight, "sub").reshape(t_block, 2 * cols)

    video_inv = inv_rms(video_group)
    video_hat = video_group * video_inv
    attn_scale1 = 1.0 + pick_rows(group_hot, scale_rows)
    normed = (video_hat * (attn_gain_f * attn_scale1)).astype(BF)
    qkv_pre = dot(normed, qkv_weight)
    query_pre = qkv_pre[:, :cols]
    key_pre = qkv_pre[:, cols : 2 * cols]
    flow = Flow(
        total_rows(
            jnp.stack([jnp.sum(query_pre * query_pre, 1), jnp.sum(key_pre * key_pre, 1)])
        )
    )
    order.step(flow)
    inverse = lax.rsqrt(flow.result / width + epsilon)
    query_inv = inverse[0].reshape(group, 1)
    key_inv = inverse[1].reshape(group, 1)
    query_hat = query_pre * query_inv
    key_hat = key_pre * key_inv
    cosine, sine = rope_tables(group_pos, head_dim, heads)
    queries = (rotate(query_hat * query_gain_f, cosine, sine).astype(BF) * score_scale).astype(BF)
    keys = rotate(key_hat * key_gain_f, cosine, sine).astype(BF)
    values = qkv_pre[:, 2 * cols :].astype(BF)
    lanes = 2 * head_dim if heads % 2 == 0 else head_dim
    parts = [slice(i * lanes, (i + 1) * lanes) for i in range(cols // lanes)]
    kv = gather_rows(order.tie(jnp.concatenate([keys, values], 1))[0], "seq")

    units = gate_weight.shape[1] // num_seq
    gate_up = jnp.stack(
        [
            jnp.concatenate(
                [w[:, i * units : (i + 1) * units] for w in (gate_weight, up_weight)], 1
            )
            for i in range(num_seq)
        ]
    )
    (gate_up,) = order.tie(gate_up)
    gate_up = swap_blocks(gate_up, "seq").reshape(num_seq * w_rows, 2 * units)
    gate_up = gather_rows(lax.optimization_barrier((gate_up, kv))[0], "sub")
    gate_up = (
        gate_up.reshape(num_sub, num_seq, w_rows, 2 * units)
        .transpose(1, 0, 2, 3)
        .reshape(width, 2 * units)
    )
    down_block = lax.optimization_barrier((down_weight, text_weight))[0]
    down_block = gather_rows(down_block, "sub")

    slots = cap_total // num_seq
    text_parts = {}

    def text_chain():
        part = dot(cap_block, text_weight).astype(BF)
        pre = yield from scatter_seq(part)
        key_pre = pre[:, :cols]
        square = yield from total(jnp.sum(key_pre * key_pre, 1)[None], ("sub",))
        inv = lax.rsqrt(square / width + epsilon).reshape(slots, 1)
        text_parts["inv"], text_parts["hat"] = inv, key_pre * inv
        gain = lax.dynamic_slice_in_dim(
            late_flow.result[3 * clips : 3 * clips + 1], sub * cols, cols, 1
        )
        text_parts["gain"] = gain
        gathered = yield from gather_seq(
            jnp.concatenate([(key_pre * inv * gain).astype(BF), pre[:, cols:].astype(BF)], 1)
        )
        return gathered

    for _ in range(len(axis_bits("seq")) + len(axis_bits("sub")) - 3):
        order.step(late_flow)
    text_flow = Flow(text_chain())
    for _ in range(3):
        order.step(late_flow, text_flow)
    self_out, lse = order.step(
        text_flow,
        work=lambda *a: self_forward(ranges, *a, meta, head_dim, lanes, rows),
        args=(queries, kv),
    )
    while not (text_flow.done and late_flow.done):
        order.step(text_flow, late_flow)
    tkv = text_flow.result
    text_inv, text_hat, text_key_gain_f = (text_parts[k] for k in ("inv", "hat", "gain"))
    late = late_flow.result
    attn_gate = pick_rows(own_hot, late[:clips])
    ffn_scale = pick_rows(own_hot, late[clips : 2 * clips])
    ffn_gate = pick_rows(own_hot, late[2 * clips : 3 * clips])
    attn_out_f = late[3 * clips + 1 : 3 * clips + 2]
    ffn_gain_f = late[3 * clips + 2 : 3 * clips + 3]
    ffn_out_f = late[3 * clips + 3 : 3 * clips + 4]

    mixed_heads, cross_out, cross_lse = cross_forward(
        ranges, gates, queries, tkv, meta, self_out, head_dim, lanes
    )
    flow = Flow(swap_direct([mixed_heads[i * rows : (i + 1) * rows] for i in range(num_sub)]))
    order.step(flow)
    mixed = jnp.concatenate(in_order(flow.result, sub), 1)

    def run(flow):
        while not flow.done:
            order.step(flow)
        return flow.result

    video_own = video.astype(F32)
    projected = dot(mixed, out_full)
    proj_inv = inv_rms(projected)
    proj_hat = projected * proj_inv
    attn_tanh = jnp.tanh(attn_gate)
    hidden_state = video_own + attn_tanh * proj_hat * attn_out_f
    hidden_inv = inv_rms(hidden_state)
    hidden_hat = hidden_state * hidden_inv
    ffn_mult = ffn_gain_f * (1.0 + ffn_scale)
    ffn_in = jnp.concatenate(run(Flow(gather_even_odd((hidden_hat * ffn_mult).astype(BF)))), 0)
    half = ffn_in.shape[0] // 2
    gate_up_pre = dot(ffn_in, gate_up)
    gate_pre = gate_up_pre[:, :units]
    up_pre = gate_up_pre[:, units:]
    gate_sig = jax.nn.sigmoid(gate_pre)
    gate_act = gate_pre * gate_sig
    activated = (gate_act * up_pre).astype(BF)
    down_part = dot(activated, down_block).astype(BF)
    down_out = run(Flow(scatter_even_odd(down_part[:half], down_part[half:])))
    down_inv = inv_rms(down_out)
    down_hat = down_out * down_inv
    ffn_tanh = jnp.tanh(ffn_gate)
    block_out = (hidden_state + ffn_tanh * down_hat * ffn_out_f).astype(BF)

    grad_out = cotangent.astype(F32)
    ffn_gate_grad = grad_out * down_hat * ffn_out_f * (1.0 - ffn_tanh * ffn_tanh)
    ffn_out_gain_part = jnp.sum(grad_out * ffn_tanh * down_hat, 0)
    down_grad = norm_back(down_hat, down_inv, grad_out * ffn_tanh * ffn_out_f).astype(BF)
    down_grad = jnp.concatenate(run(Flow(gather_even_odd(down_grad))), 0)
    act_grad = dot_nt(down_grad, down_block)
    gate_grad = (act_grad * up_pre * gate_sig * (1.0 + gate_pre * (1.0 - gate_sig))).astype(BF)
    up_grad = (act_grad * gate_act).astype(BF)
    gate_up_grad = jnp.concatenate([gate_grad, up_grad], 1)
    ffn_in_part = dot_nt(gate_up_grad, gate_up).astype(BF)
    ffn_in_grad = run(Flow(scatter_even_odd(ffn_in_part[:half], ffn_in_part[half:])))
    down_weight_term = dot_tn(activated, down_grad).astype(BF)
    down_weight_grad = scatter_rows(down_weight_term, "sub").astype(F32)
    gate_up_term = dot_tn(ffn_in, gate_up_grad).astype(BF)
    gate_up_term = (
        gate_up_term.reshape(num_seq, num_sub, w_rows, 2 * units)
        .transpose(1, 0, 2, 3)
        .reshape(width, 2 * units)
    )
    gate_up_term = scatter_rows(gate_up_term, "sub").reshape(num_seq, w_rows, 2 * units)

    ffn_gain_part = jnp.sum(ffn_in_grad * hidden_hat * (1.0 + ffn_scale), 0)
    ffn_scale_grad = ffn_in_grad * hidden_hat * ffn_gain_f
    hidden_grad = grad_out + norm_back(hidden_hat, hidden_inv, ffn_in_grad * ffn_mult)
    attn_gate_grad = hidden_grad * proj_hat * attn_out_f * (1.0 - attn_tanh * attn_tanh)
    attn_out_gain_part = jnp.sum(hidden_grad * attn_tanh * proj_hat, 0)
    proj_grad = norm_back(proj_hat, proj_inv, hidden_grad * attn_tanh * attn_out_f).astype(BF)
    mixed_grad = dot_nt(proj_grad, out_full).astype(BF)
    out_weight_term = dot_tn(mixed, proj_grad).astype(BF)
    flow = Flow(swap_direct(blocks_for(mixed_grad, 1)))
    order.step(flow)
    dout = jnp.concatenate(flow.result, 0)
    cross_gate_part = jnp.sum(
        (dout.astype(F32) * cross_out).reshape(group, heads, head_dim), (0, 2)
    ) * (1.0 - gates * gates)

    def clip_sums(values):
        return dot_tn(own_hot.astype(BF), values.astype(BF))

    def at_columns(part):
        return lax.dynamic_update_slice_in_dim(
            jnp.zeros((1, width), F32), part.reshape(1, -1), sub * cols, 1
        )

    gate_row = lax.dynamic_update_slice_in_dim(
        jnp.zeros((1, width), F32), cross_gate_part.reshape(1, -1), sub * heads, 1
    )
    late_flow = Flow(
        total_cube(
            jnp.concatenate(
                [
                    clip_sums(attn_gate_grad),
                    clip_sums(ffn_scale_grad),
                    clip_sums(ffn_gate_grad),
                    attn_out_gain_part[None],
                    ffn_gain_part[None],
                    ffn_out_gain_part[None],
                    gate_row,
                ],
                0,
            ),
            ("seq", "sub"),
        )
    )
    query_start, dtkv = cross_backward(
        ranges, gates, queries, tkv, meta, dout, cross_lse, head_dim, lanes
    )
    text_flow = Flow(scatter_seq(dtkv))
    def text_back_chain():
        reduced = yield from scatter_seq(dtkv)
        low = reduced[:, :cols].astype(BF).astype(F32)
        hat_grad = low * text_key_gain_f
        inner = yield from total(jnp.sum(text_hat * hat_grad, 1)[None], ("sub",))
        text_parts["gain"] = jnp.sum(low * text_hat, 0)
        pre_grad = text_inv * (hat_grad - text_hat * (inner / width).reshape(slots, 1))
        gathered = yield from gather_seq(
            jnp.concatenate([pre_grad.astype(BF), reduced[:, cols:].astype(BF)], 1)
        )
        return gathered

    text_flow = Flow(text_back_chain())
    query_rot_grad, dkv = order.step(
        text_flow,
        late_flow,
        work=lambda *a: self_backward(ranges, a[0], a[1], meta, *a[2:], head_dim, lanes, rows),
        args=(queries, kv, dout, self_out, lse, query_start),
    )
    dkv = scatter_rows(dkv, "seq")
    out_weight_term = lax.optimization_barrier((out_weight_term, dkv))[0]
    out_weight_term = scatter_rows(out_weight_term, "seq").reshape(num_sub, w_rows, width)
    out_weight_grad = jnp.sum(swap_blocks(out_weight_term, "sub").astype(F32), 0)
    while not (text_flow.done and late_flow.done):
        order.step(text_flow, late_flow)
    text_key_gain_part = text_parts["gain"]
    text_grad = text_flow.result
    query_rot_grad = query_rot_grad.astype(BF).astype(F32)
    key_rot_grad = dkv[:, :cols].astype(F32)
    value_grad = dkv[:, cols:]
    query_norm_grad = rotate(query_rot_grad, cosine, -sine)
    query_gain_part = jnp.sum(query_norm_grad * query_hat, 0)
    query_hat_grad = query_norm_grad * query_gain_f
    key_norm_grad = rotate(key_rot_grad, cosine, -sine)
    key_gain_part = jnp.sum(key_norm_grad * key_hat, 0)
    key_hat_grad = key_norm_grad * key_gain_f
    flow = Flow(
        total_rows(
            jnp.stack(
                [jnp.sum(query_hat * query_hat_grad, 1), jnp.sum(key_hat * key_hat_grad, 1)]
            )
        )
    )
    order.step(flow)
    inner = flow.result / width
    caption_part = dot_nt(text_grad, text_weight).astype(BF).reshape(num_sub, cap_shard, t_block)
    text_term = dot_tn(cap_block, text_grad).astype(BF).reshape(num_sub, t_rows, 2 * cols)
    query_pre_grad = query_inv * (query_hat_grad - query_hat * inner[0].reshape(group, 1))
    key_pre_grad = key_inv * (key_hat_grad - key_hat * inner[1].reshape(group, 1))
    qkv_grad = jnp.concatenate([query_pre_grad.astype(BF), key_pre_grad.astype(BF), value_grad], 1)
    qkv_term = dot_tn(normed, qkv_grad).astype(BF)
    normed_part = dot_nt(qkv_grad, qkv_weight)

    hat_grad = normed_part * video_hat
    attn_gain_part = jnp.sum(hat_grad * attn_scale1, 0)
    scale_part = dot_tn(group_hot.astype(BF), (hat_grad * attn_gain_f).astype(BF))
    early_flow = Flow(
        total(
            jnp.concatenate(
                [
                    scale_part,
                    attn_gain_part[None],
                    at_columns(query_gain_part),
                    at_columns(key_gain_part),
                    at_columns(text_key_gain_part),
                ],
                0,
            ),
            ("seq", "sub"),
        )
    )
    qkv_flow = Flow(scatter_seq(qkv_term))
    caption_block = jnp.sum(
        swap_blocks(order.tie(caption_part)[0], "sub").astype(F32), 0
    ).astype(BF)
    normed_low = jnp.concatenate(blocks_for(normed_part.astype(BF), 0), 0)
    normed_grad = scatter_rows(order.tie(normed_low)[0], "sub").astype(F32)
    text_term = lax.optimization_barrier((text_term, normed_grad))[0]
    text_term = swap_blocks(text_term, "sub")
    caption_flow = Flow(gather_seq(caption_block, 1, F32))
    order.step(early_flow, qkv_flow)
    order.step(early_flow, qkv_flow)
    order.step(early_flow)
    late_sum = late_flow.result
    early_sum = early_flow.result
    mod_low = jnp.concatenate(
        [
            early_sum[:clips],
            late_sum[:clips],
            late_sum[clips : 2 * clips],
            late_sum[2 * clips : 3 * clips],
        ],
        1,
    ).astype(BF)
    cond_part = lax.dynamic_update_slice_in_dim(
        jnp.zeros(conditioning.shape, F32), dot_nt(mod_low, ada_weight), device * cond_rows, 1
    )
    cond_flow = Flow(total(cond_part, ("seq", "sub")))
    qkv_term = order.tie(qkv_flow.result.astype(BF).reshape(num_sub, w_rows, 3 * cols))[0]
    qkv_term = swap_blocks(qkv_term, "sub")
    order.step(caption_flow)
    order.step(cond_flow, caption_flow)
    order.step(cond_flow)
    order.step(cond_flow)
    caption_grad = caption_flow.result
    query_weight_grad, key_weight_grad, value_weight_grad = (
        jnp.concatenate([block[:, j * cols : (j + 1) * cols] for block in qkv_term], 1).astype(F32)
        for j in range(3)
    )
    text_key_weight_grad, text_value_weight_grad = (
        jnp.concatenate([block[:, j * cols : (j + 1) * cols] for block in text_term], 1).astype(F32)
        for j in range(2)
    )
    gate_up_term = swap_blocks(gate_up_term, "seq")
    gate_weight_grad, up_weight_grad = (
        jnp.concatenate(
            [gate_up_term[i, :, j * units : (j + 1) * units] for i in range(num_seq)], 1
        ).astype(F32)
        for j in range(2)
    )

    own_hat, own_inv, own_scale1 = video_hat[:rows], video_inv[:rows], attn_scale1[:rows]
    video_grad = hidden_grad + norm_back(own_hat, own_inv, normed_grad * (attn_gain_f * own_scale1))

    def own_gain(row):
        return lax.dynamic_slice_in_dim(row, device * gain_rows, gain_rows, 0)

    bias_rows = ada_bias.shape[0]
    ada_bias_grad = jnp.sum(
        lax.dynamic_slice_in_dim(mod_low.astype(F32), device * bias_rows, bias_rows, 1), 0
    )
    ada_weight_grad = dot_tn(cond_slice, mod_low)
    cond_sig = jax.nn.sigmoid(cond_float)
    cond_grad = cond_flow.result * cond_sig * (1.0 + cond_float * (1.0 - cond_sig))
    return (
        block_out,
        video_grad,
        caption_grad,
        cond_grad,
        ada_weight_grad,
        ada_bias_grad,
        query_weight_grad,
        key_weight_grad,
        value_weight_grad,
        out_weight_grad,
        text_key_weight_grad,
        text_value_weight_grad,
        gate_weight_grad,
        up_weight_grad,
        down_weight_grad,
        own_gain(early_sum[clips]),
        own_gain(early_sum[clips + 1]),
        own_gain(early_sum[clips + 2]),
        own_gain(early_sum[clips + 3]),
        own_gain(late_sum[3 * clips]),
        own_gain(late_sum[3 * clips + 1]),
        own_gain(late_sum[3 * clips + 2]),
        late_sum[3 * clips + 3, :heads_total],
    )


def solution(mesh):
    matrix = P(BOTH, None)
    vector = P(BOTH)
    return jax.shard_map(
        body,
        mesh=mesh,
        in_specs=(matrix, P(), P("sub", None), P(), P(), matrix, matrix, vector)
        + (matrix,) * 9
        + (vector,) * 7
        + (P(), matrix),
        out_specs=(matrix, matrix, P("sub", None), P(), matrix, vector)
        + (matrix,) * 9
        + (vector,) * 7
        + (P(),),
        check_vma=False,
    )
```
